128 devices in a mesh: rep: 8 (over y, core), head: 16 (over z, x).
Axes of the slice: x: 4, y: 4, z: 4, core: 2. Of those that a mesh axis runs over, the one named last changes fastest.
Arguments:
- prefill_states: bfloat16 [256, 2, 128, 64, 128], P('rep', None, 'head'), may hold values from -6 to 6
- inner_tail: bfloat16 [256, 2, 3, 8192], P('rep', None, None, 'head'), may hold values from -6 to 6
- group_tail: bfloat16 [256, 2, 3, 2048], P('rep'), may hold values from -6 to 6
- assignment: int32 [256, 1], P('rep'), may hold values from 0 to 31; in each aligned block of 32 rows (0 to 31, 32 to 63, ...) at most 2 rows name the same one
- decode_inner: bfloat16 [8, 16, 8, 2, 2, 2, 2048], P('rep', 'head'), may hold values from -6 to 6
- decode_groups: bfloat16 [8, 4, 8, 2, 2, 2, 2048], P('rep'), may hold values from -6 to 6
- decode_rate: bfloat16 [8, 16, 8, 2, 2, 2, 32], P('rep', 'head'), may hold values from -3 to 3
- conv_inner: float32 [2, 4, 8192], replicated, may hold values from -3 to 3
- conv_group: float32 [2, 4, 2048], replicated, may hold values from -3 to 3
- bias_inner: float32 [2, 8192], replicated, may hold values from -3 to 3
- bias_group: float32 [2, 2048], replicated, may hold values from -3 to 3
- rate_bias: float32 [2, 128], replicated, may hold values from -4 to -1
- decay_log: float32 [2, 128], replicated, may hold values from 0 to 2.8
- skip_gain: float32 [2, 128], replicated, may hold values from 0.5 to 2
Outputs:
- decoded: bfloat16 [8, 16, 8, 2, 2, 2, 2048], P('rep', 'head')
The draws below stay inside these ranges and needn't reach their ends.
Inputs may be any that keep to these rules, and one draw needn't show every extreme that they name: `assignment`: the 32 requests of one index of rep name any one replica at most 2 times, a bound that some block reaches.
All inputs are finite; a program needn't handle non-finite values.
Results may differ from the reference program's by a relative error of at most 0.001.
Values may be sent and summed in bfloat16 or wider, within the bound.
No kernel may reach another device: no remote copies, remote signals or barrier semaphores. Data moves between devices by JAX's collectives and lax.ppermute only.
A program may use at most 128 MiB of HBM per device.

```python
import math
import jax
import jax.numpy as jnp
import numpy as np
from jax import lax

HEADS = 128
HEAD_DIM = 64
STATE = 128
GROUPS = 8
KERNEL = 4
TP = 4
LAYERS = 2
STEPS = 2
REQ_ROW = 32
REQS = 256
SUBS = 4
REPLICAS = 32
CAP = 2
HEAD_RANK = 2
D_INNER = 8192
BC_WIDTH = 2048
N_REP = 8
N_HEAD = 16


def level_of(rng, shape, pieces, smallest, high):
    factor_of = 1.0
    for dim, blocks in pieces:
        draws = jax.random.uniform(jax.random.fold_in(jax.random.fold_in(rng, 6), dim), (blocks,), jnp.float32, smallest / len(pieces), high / len(pieces))
        factor_of = factor_of * jnp.repeat(jnp.exp(draws), shape[dim] // blocks).reshape((-1,) + (1,) * (len(shape) - 1 - dim))
    return factor_of


def shared_out(stream_key, own, number, rows, amount, top, most, lean):
    ranking = jax.random.permutation(stream_key, amount)
    packed, common = load_shares(amount, rows * top, most, lean, True), load_shares(amount, rows * top, most, lean, False)
    places = jnp.arange(amount)

    def named(lengths, turn):
        used = int((lengths > 0).sum())
        fixed = max(1, used // 4)
        shifted = fixed + (places - fixed + turn * (used - fixed)) % max(1, amount - fixed)
        return jnp.zeros((amount,), jnp.int32).at[ranking[jnp.where(places < fixed, places, shifted)]].set(jnp.asarray(lengths, jnp.int32))

    lengths = jnp.where(number % 4 == 0, named(packed, number // 4), named(common, number - number // 4 - 1))
    mixed = jax.random.permutation(jax.random.fold_in(own, 3), amount)
    giver, receiver = mixed[0:amount // 2 * 2:2], mixed[1:amount // 2 * 2:2]
    slack = jnp.minimum(lengths[giver] - 1, most - lengths[receiver]) // 2
    slack = jnp.where((giver == ranking[0]) | (receiver == ranking[0]) | (lengths[receiver] == 0), 0, jnp.maximum(slack, 0))
    shifted = jax.random.randint(jax.random.fold_in(own, 4), (amount // 2,), 0, 1 << 20) % (slack + 1)
    lengths = lengths.at[giver].add(-shifted).at[receiver].add(shifted)
    items = jnp.searchsorted(jnp.cumsum(lengths), jnp.arange(rows * top), side="right").astype(jnp.int32)
    listing = items.reshape(top, rows).T
    listing = listing[jax.random.permutation(jax.random.fold_in(own, 1), rows)]
    turn = jax.random.randint(jax.random.fold_in(own, 2), (rows, 1), 0, top)
    return jnp.take_along_axis(listing, (jnp.arange(top)[None, :] + turn) % top, axis=1)


def load_shares(count, total, reach, slope, full):
    weights = [(1 << 20) // math.isqrt(standing ** slope) + 1 for standing in range(1, count + 1)]
    largest = reach if full else min(reach, max(-(-total // count), total * weights[0] // sum(weights)))
    least = 1 if total - largest >= count - 1 else 0
    counts, rest = [largest] + [least] * (count - 1), total - largest - least * (count - 1)
    while rest > 0:
        candidates = [i for i in range(1, count) if counts[i] < largest] or [i for i in range(1, count) if counts[i] < reach]
        mass, budget = sum([weights[i] for i in candidates]), rest
        for i in candidates:
            addition = min(reach - counts[i], max(1, budget * weights[i] // mass), rest)
            counts[i] = counts[i] + addition
            rest = rest - addition
    return np.array(counts)


def gaussian(stream_key, extent, scale, limit, cuts=(), held_as=jnp.bfloat16):
    result = jax.random.normal(stream_key, extent, jnp.float32) * scale
    if len(cuts) > 0:
        result = level_of(stream_key, extent, cuts, -0.22, 0.18) * result
    return jnp.clip(result, min=-limit, max=limit).astype(held_as)


def setup_inputs(seed: int = 0) -> dict:
    streams_of = jax.random.split(jax.random.key(seed), 15)
    prefill_states = gaussian(streams_of[0], (REQS, LAYERS, HEADS, HEAD_DIM, STATE), 1.0, 6.0, ((0, 8), (2, 16)))
    inner_tail = gaussian(streams_of[1], (REQS, LAYERS, KERNEL - 1, D_INNER), 1.0, 6.0, ((0, 8), (3, 16)))
    group_tail = gaussian(streams_of[2], (REQS, LAYERS, KERNEL - 1, BC_WIDTH), 1.0, 6.0, ((0, 8),))
    assignment_keys = jax.random.split(jax.random.fold_in(streams_of[3], 1), REQS // REQ_ROW)
    assignment_turns = jax.random.permutation(jax.random.fold_in(streams_of[3], 3), REQS // REQ_ROW)
    assignment = jax.vmap(lambda own, number: shared_out(jax.random.fold_in(streams_of[3], 2), own, number, REQ_ROW, REPLICAS, 1, CAP, 2))(assignment_keys, assignment_turns).reshape((REQS, 1))
    decode_inner = gaussian(streams_of[4], (N_REP, N_HEAD, N_REP, CAP, LAYERS, STEPS, N_HEAD * HEAD_RANK * HEAD_DIM), 1.0, 6.0, ((0, 8), (1, 16)))
    decode_groups = gaussian(streams_of[5], (N_REP, SUBS, N_REP, CAP, LAYERS, STEPS, BC_WIDTH), 1.0, 6.0, ((0, 8),))
    decode_rate = gaussian(streams_of[6], (N_REP, N_HEAD, N_REP, CAP, LAYERS, STEPS, N_HEAD * HEAD_RANK), 0.5, 3.0, ((0, 8), (1, 16)))
    conv_inner = gaussian(streams_of[7], (LAYERS, KERNEL, D_INNER), KERNEL ** -0.5, 3.0, (), jnp.float32)
    conv_group = gaussian(streams_of[8], (LAYERS, KERNEL, BC_WIDTH), KERNEL ** -0.5, 3.0, (), jnp.float32)
    bias_inner = gaussian(streams_of[9], (LAYERS, D_INNER), 0.5, 3.0, (), jnp.float32)
    bias_group = gaussian(streams_of[10], (LAYERS, BC_WIDTH), 0.5, 3.0, (), jnp.float32)
    rate_bias = jnp.clip(jax.random.uniform(streams_of[11], (LAYERS, HEADS), jnp.float32, -4.0, -1.0), -4.0, -1.0)
    decay_log = jnp.clip(jax.random.uniform(streams_of[12], (LAYERS, HEADS), jnp.float32, 0.0, 2.8), 0.0, 2.8)
    skip_gain = jnp.clip(jnp.exp(jax.random.uniform(streams_of[13], (LAYERS, HEADS), jnp.float32, math.log(0.5), math.log(2.0))), 0.5, 2.0)
    return dict(prefill_states=prefill_states, inner_tail=inner_tail, group_tail=group_tail, assignment=assignment, decode_inner=decode_inner, decode_groups=decode_groups, decode_rate=decode_rate, conv_inner=conv_inner, conv_group=conv_group, bias_inner=bias_inner, bias_group=bias_group, rate_bias=rate_bias, decay_log=decay_log, skip_gain=skip_gain)


def conv_update(history, fresh, weight, offset):
    window = jnp.concatenate([history, fresh[..., None, :]], axis=-2)
    summed = jnp.sum(weight * window.astype(jnp.float32), axis=-2) + offset
    return jax.nn.silu(summed), window[..., 1:, :]


def state_step(states, inner_act, write_vec, read_vec, rate_raw, rate_shift, damping_log, skip_part):
    step_size = jax.nn.softplus(rate_raw.astype(jnp.float32) + rate_shift)
    damping = jnp.exp(-step_size * jnp.exp(damping_log))
    states = damping[..., None, None] * states + (step_size[..., None] * inner_act)[..., None] * write_vec[..., None, None, :]
    output = jnp.einsum("...upn,...n->...up", states, read_vec, precision=lax.Precision.HIGHEST) + skip_part[..., None] * inner_act
    return states, output


def spread_groups(vector, repeat_count):
    shaped = vector.reshape(vector.shape[:-1] + (GROUPS, STATE))
    return jnp.repeat(shaped, repeat_count, axis=-2)


def slot_sources(assignment, replica):
    chosen = assignment[:, 0].reshape(N_REP, REQ_ROW)
    order = jnp.arange(REQ_ROW, dtype=jnp.int32)
    same = chosen[:, :, None] == chosen[:, None, :]
    before = order[None, :] < order[:, None]
    rank_in = jnp.sum((same & before[None]).astype(jnp.int32), axis=2)
    match = (chosen[:, None, :] == replica) & (rank_in[:, None, :] == jnp.arange(CAP, dtype=jnp.int32)[None, :, None])
    present = jnp.any(match, axis=2)
    within = jnp.sum(match.astype(jnp.int32) * order[None, None, :], axis=2)
    rows_at = jnp.arange(N_REP, dtype=jnp.int32)[:, None] * REQ_ROW + within
    return rows_at, present


def reference(prefill_states, inner_tail, group_tail, assignment, decode_inner, decode_groups, decode_rate, conv_inner, conv_group, bias_inner, bias_group, rate_bias, decay_log, skip_gain):
    group_span = GROUPS * STATE
    zero_half = jnp.zeros((), jnp.bfloat16)
    layer_outs = []
    for layer_idx in range(LAYERS):
        def one_replica(replica):
            rows_at, present = slot_sources(assignment, replica)
            home = replica // SUBS
            sub_idx = replica % SUBS
            states = prefill_states[rows_at, layer_idx].astype(jnp.float32)
            states = jnp.where(present[:, :, None, None, None], states, 0.0)
            states = states.reshape(N_REP, CAP, N_HEAD, TP, HEAD_RANK, HEAD_DIM, STATE)
            inner_hist = jnp.where(present[:, :, None, None], inner_tail[rows_at, layer_idx], zero_half)
            group_hist = jnp.where(present[:, :, None, None], group_tail[rows_at, layer_idx], zero_half)
            fresh_inner = lax.dynamic_slice_in_dim(decode_inner[home], sub_idx * TP, TP, 0)[:, :, :, layer_idx]
            fresh_inner = fresh_inner.reshape(TP, N_REP, CAP, STEPS, N_HEAD, HEAD_RANK * HEAD_DIM)
            fresh_inner = fresh_inner.transpose(1, 2, 3, 4, 0, 5).reshape(N_REP, CAP, STEPS, D_INNER)
            fresh_rate = lax.dynamic_slice_in_dim(decode_rate[home], sub_idx * TP, TP, 0)[:, :, :, layer_idx]
            fresh_rate = fresh_rate.reshape(TP, N_REP, CAP, STEPS, N_HEAD, HEAD_RANK).transpose(1, 2, 3, 4, 0, 5)
            fresh_group = decode_groups[home, sub_idx][:, :, layer_idx]
            rate_shift = rate_bias[layer_idx].reshape(N_HEAD, TP, HEAD_RANK)
            damping_log = decay_log[layer_idx].reshape(N_HEAD, TP, HEAD_RANK)
            skip_part = skip_gain[layer_idx].reshape(N_HEAD, TP, HEAD_RANK)
            results = []
            for step_idx in range(STEPS):
                inner_act, inner_hist = conv_update(inner_hist, fresh_inner[:, :, step_idx], conv_inner[layer_idx], bias_inner[layer_idx])
                group_act, group_hist = conv_update(group_hist, fresh_group[:, :, step_idx], conv_group[layer_idx], bias_group[layer_idx])
                write_vec = spread_groups(group_act[..., :group_span], N_HEAD // GROUPS)
                read_vec = spread_groups(group_act[..., group_span:], N_HEAD // GROUPS)
                write_vec = jnp.broadcast_to(write_vec[:, :, :, None, :], (N_REP, CAP, N_HEAD, TP, STATE))
                read_vec = jnp.broadcast_to(read_vec[:, :, :, None, :], (N_REP, CAP, N_HEAD, TP, STATE))
                inner_heads = inner_act.reshape(N_REP, CAP, N_HEAD, TP, HEAD_RANK, HEAD_DIM)
                states, output = state_step(states, inner_heads, write_vec, read_vec, fresh_rate[:, :, step_idx], rate_shift, damping_log, skip_part)
                results.append(output.transpose(3, 0, 1, 2, 4, 5).reshape(TP, N_REP, CAP, N_HEAD * HEAD_RANK * HEAD_DIM))
            return jnp.stack(results, axis=3).astype(jnp.bfloat16)

        mapped = lax.map(one_replica, jnp.arange(REPLICAS, dtype=jnp.int32))
        layer_outs.append(mapped.reshape(N_REP, N_HEAD, N_REP, CAP, STEPS, N_HEAD * HEAD_RANK * HEAD_DIM))
    return jnp.stack(layer_outs, axis=4)
```

```python
import jax
import jax.numpy as jnp
from jax import lax
from jax.experimental import pallas as pl
from jax.experimental.pallas import tpu as pltpu
from jax.sharding import PartitionSpec as P

F32 = jnp.float32
BF16 = jnp.bfloat16
AXES = ("rep", "head")
N_REP, N_HEAD, TP, CAP, LAYERS, STEPS, KERNEL = 8, 16, 4, 2, 2, 2, 4
SUBS = N_HEAD // TP
REPLICAS = N_REP * SUBS
REQ = 32
HEADS = 128
HEADS_LOCAL = HEADS // N_HEAD
HEAD_DIM, STATE = 64, 128
WIDTH = HEADS_LOCAL * HEAD_DIM
RANK_WIDTH = WIDTH // TP
GROUP_SPAN = 1024
ROWS = CAP * LAYERS * STEPS
SLOT_ROWS = REPLICAS * ROWS
REQ_ROWS = REQ * LAYERS * STEPS
HIST_ROWS = REQ * (KERNEL - 1) * LAYERS
VMEM = pl.BlockSpec(memory_space=pltpu.VMEM)
HBM = pl.BlockSpec(memory_space=pltpu.HBM)


def iota(shape, dim):
    return lax.broadcasted_iota(jnp.int32, shape, dim)


def one_hot(cond):
    return jnp.where(cond, 1.0, 0.0).astype(BF16)


def dot(a, b):
    return jnp.dot(a, b, preferred_element_type=F32)


def split3(v):
    hi = v.astype(BF16)
    rest = v - hi.astype(F32)
    mid = rest.astype(BF16)
    return hi, mid, (rest - mid.astype(F32)).astype(BF16)


def pack_kernel(
    inner_hbm,
    group_hbm,
    rate_hbm,
    inner_tail_hbm,
    group_tail_hbm,
    chosen_hbm,
    conv_inner_hbm,
    conv_group_hbm,
    bias_inner_hbm,
    bias_group_hbm,
    rate_bias_hbm,
    decay_hbm,
    skip_hbm,
    states_hbm,
    out_ref,
    states_ref,
    part_ref,
    place_ref,
    taps_ref,
    params_ref,
    inner_buf,
    group_buf,
    rate_ref,
    rate_buf,
    hist_buf,
    inner_tail_ref,
    tail_b_ref,
    tail_c_ref,
    chosen_ref,
    conv_inner_ref,
    conv_b_ref,
    conv_c_ref,
    bias_inner_ref,
    bias_b_ref,
    bias_c_ref,
    rate_bias_ref,
    decay_ref,
    skip_ref,
    sems,
):
    pos = lax.axis_index("head")
    sub, rank = lax.div(pos, TP), lax.rem(pos, TP)
    quarter = group_hbm.at[0, sub, :, lax.div(rank, LAYERS), lax.rem(rank, LAYERS)]
    copies = [
        pltpu.make_async_copy(src, dst, sems.at[13 + n])
        for n, (src, dst) in enumerate(
            ((rate_hbm.at[0, 0], rate_ref), (quarter, group_buf), (inner_hbm.at[0, 0], inner_buf))
        )
    ]
    for copy in copies:
        copy.start()
    inner = pl.ds(pl.multiple_of(pos * WIDTH, WIDTH), WIDTH)
    b = pl.ds(pl.multiple_of(lax.div(pos, 2) * STATE, STATE), STATE)
    c = pl.ds(pl.multiple_of(GROUP_SPAN + lax.div(pos, 2) * STATE, STATE), STATE)
    moves = (
        (chosen_hbm, chosen_ref),
        (inner_tail_hbm, inner_tail_ref),
        (group_tail_hbm.at[:, :, :, b], tail_b_ref),
        (group_tail_hbm.at[:, :, :, c], tail_c_ref),
        (conv_inner_hbm.at[:, :, inner], conv_inner_ref),
        (conv_group_hbm.at[:, :, b], conv_b_ref),
        (conv_group_hbm.at[:, :, c], conv_c_ref),
        (bias_inner_hbm.at[:, inner], bias_inner_ref),
        (bias_group_hbm.at[:, b], bias_b_ref),
        (bias_group_hbm.at[:, c], bias_c_ref),
        (rate_bias_hbm, rate_bias_ref),
        (decay_hbm, decay_ref),
        (skip_hbm, skip_ref),
    )
    tails = [pltpu.make_async_copy(src, dst, sems.at[n]) for n, (src, dst) in enumerate(moves)]
    for copy in tails:
        copy.start()
    near = pltpu.make_async_copy(states_hbm, states_ref, sems.at[16])
    near.start()
    turn = (iota((ROWS, 128), 0) - 2 * rank) & 7
    copies[0].wait()
    for r in range(N_REP):
        rate_buf[r * ROWS : (r + 1) * ROWS] = jnp.concatenate(
            [rate_ref[r, c, l].astype(F32) for c in range(CAP) for l in range(LAYERS)], axis=0
        )
    rates = rate_buf[...].astype(BF16)
    rate_rows = jnp.zeros((N_HEAD, N_REP * 128), F32)
    for u in range(2):
        pick = one_hot(iota((N_HEAD, 2 * N_HEAD), 1) == 2 * iota((N_HEAD, 2 * N_HEAD), 0) + u)
        turned = lax.dot_general(
            pick, rates, (((1,), (1,)), ((), ())), preferred_element_type=F32
        ).astype(BF16)
        shape = (N_REP * ROWS, N_REP * 128)
        row, lane = iota(shape, 0), iota(shape, 1)
        place = one_hot(
            (row // ROWS == lane // 128) & (lane % 128 == 2 * (row % ROWS) + u)
        )
        rate_rows = rate_rows + dot(turned, place)
    copies[1].wait()
    copies[2].wait()
    for r in range(N_REP):
        inner = jnp.concatenate(
            [inner_buf[r, c, l].astype(F32) for c in range(CAP) for l in range(LAYERS)], axis=0
        ).astype(BF16)
        fresh = group_buf[r].astype(F32)
        for h in range(N_HEAD):
            out_ref[r, h, 0:ROWS, :] = inner[:, h * 128 : (h + 1) * 128]
            at = (h // 2) * 128
            b_new = fresh[:, at : at + 128]
            c_new = fresh[:, GROUP_SPAN + at : GROUP_SPAN + at + 128]
            tile = jnp.where(turn == 0, b_new[0:1], 0.0)
            tile = jnp.where(turn == 1, b_new[1:2], tile)
            tile = jnp.where(turn == 4, c_new[0:1], tile)
            tile = jnp.where(turn == 5, c_new[1:2], tile)
            tile = jnp.where(turn == 2, rate_rows[h : h + 1, r * 128 : (r + 1) * 128], tile)
            out_ref[r, h, ROWS : 2 * ROWS, :] = tile.astype(BF16)
    for copy in tails:
        copy.wait()
    for i in range(REQ):
        for j in range(KERNEL - 1):
            rows = slice((i * 3 + j) * 2, (i * 3 + j) * 2 + 2)
            hist_buf[rows, 0:WIDTH] = inner_tail_ref[i, j].astype(F32)
            hist_buf[rows, WIDTH : WIDTH + STATE] = tail_b_ref[i, j].astype(F32)
            hist_buf[rows, WIDTH + STATE :] = tail_c_ref[i, j].astype(F32)
    chosen = chosen_ref[...].astype(F32)
    ri, ci = iota((REQ, REQ), 0), iota((REQ, REQ), 1)
    column = jnp.sum(jnp.where(ri == ci, chosen, 0.0), axis=1, keepdims=True)
    before = jnp.where((column == chosen) & (ri < ci), 1.0, 0.0)
    slots = CAP * chosen + jnp.sum(before, axis=0, keepdims=True)
    slots = jnp.broadcast_to(slots, (8, REQ)).astype(BF16)
    wide = dot(slots, one_hot(iota((REQ, REQ_ROWS), 1) // 4 == iota((REQ, REQ_ROWS), 0)))[0:1]
    target = wide.astype(jnp.int32) * 4 + iota((1, REQ_ROWS), 1) % 4
    place_ref[...] = one_hot(iota((SLOT_ROWS, REQ_ROWS), 0) == target)
    wide = dot(slots, one_hot(iota((REQ, HIST_ROWS), 1) // 6 == iota((REQ, HIST_ROWS), 0)))[0:1]
    col = iota((1, HIST_ROWS), 1)
    col_key = wide.astype(jnp.int32) * 8 + (col % 2) * 4 + (col % 6) // 2
    row = iota((SLOT_ROWS, HIST_ROWS), 0)
    row_key = (row // 4) * 8 + ((row // 2) % 2) * 4 + row % 2
    hist = hist_buf[...].astype(BF16)
    second = (iota((ROWS, 1), 0) // 2) % 2 == 1
    later = iota((ROWS, 1), 0) % 2 == 1

    def by_layer(first, other):
        return jnp.where(second, other, first)

    def weight(tap):
        rows = [ref[:, tap : tap + 1, :] for ref in (conv_inner_ref, conv_b_ref, conv_c_ref)]
        return jnp.concatenate([by_layer(w[0], w[1]) for w in rows], axis=1)

    offset = jnp.concatenate(
        [by_layer(ref[0:1], ref[1:2]) for ref in (bias_inner_ref, bias_b_ref, bias_c_ref)], axis=1
    )
    total = jnp.broadcast_to(offset[None], (REPLICAS, ROWS, WIDTH + 2 * STATE))
    for tap in range(KERNEL - 1):
        window = dot(one_hot(row_key + tap == col_key), hist)
        total = total + weight(tap)[None] * window.reshape(REPLICAS, ROWS, WIDTH + 2 * STATE)
    part_ref[...] = total
    taps_ref[0] = jnp.where(later, weight(2), 0.0)
    taps_ref[1] = weight(3)
    spread = one_hot(
        iota((HEADS, WIDTH), 0) == pos * HEADS_LOCAL + iota((HEADS, WIDTH), 1) // HEAD_DIM
    )
    for n, ref in enumerate((rate_bias_ref, decay_ref, skip_ref)):
        both = by_layer(ref[0:1], ref[1:2])
        hi, mid, lo = split3(both)
        value = dot(hi, spread) + dot(mid, spread) + dot(lo, spread)
        params_ref[n] = jnp.exp(value) if n == 1 else value
    near.wait()


def step_kernel(
    got_ref,
    states_ref,
    part_ref,
    place_ref,
    taps_ref,
    params_ref,
    out_ref,
    read_buf,
    dots_buf,
    acc_buf,
    product_buf,
):
    pair = iota((1, ROWS, 128), 1) // 2
    later = iota((1, ROWS, 128), 1) % 2 == 1
    tap2_b = taps_ref[0, :, WIDTH : WIDTH + STATE][None]
    tap2_c = taps_ref[0, :, WIDTH + STATE :][None]
    tap3_b = taps_ref[1, :, WIDTH : WIDTH + STATE][None]
    tap3_c = taps_ref[1, :, WIDTH + STATE :][None]
    group = 4
    for q in range(0, REPLICAS, group):
        tiles = [got_ref[q : q + group, t, ROWS : 2 * ROWS, :].astype(F32) for t in range(TP)]
        b_new, c_new = tiles[0], tiles[2]
        for t in range(1, TP):
            b_new = jnp.where(pair == t, tiles[t], b_new)
            c_new = jnp.where(pair == t, tiles[(t + 2) % TP], c_new)
        c_new = pltpu.roll(c_new, 4, 1)
        b_act = part_ref[q : q + group, :, WIDTH : WIDTH + STATE]
        c_act = part_ref[q : q + group, :, WIDTH + STATE :]
        b_act = b_act + tap2_b * pltpu.roll(b_new, 1, 1) + tap3_b * b_new
        c_act = c_act + tap2_c * pltpu.roll(c_new, 1, 1) + tap3_c * c_new
        b_act = b_act * jax.nn.sigmoid(b_act)
        c_act = c_act * jax.nn.sigmoid(c_act)
        read_buf[q : q + group] = c_act
        same = jnp.sum(b_act * c_act, axis=2, keepdims=True)
        cross = jnp.sum(pltpu.roll(b_act, 1, 1) * c_act, axis=2, keepdims=True)
        dots_buf[0, q : q + group] = jnp.broadcast_to(same, (group, ROWS, 128))
        dots_buf[1, q : q + group] = jnp.broadcast_to(cross, (group, ROWS, 128))
    turned = read_buf[...].reshape(SLOT_ROWS, STATE).T
    hi = turned.astype(BF16)
    lo = (turned - hi.astype(F32)).astype(BF16)
    place = place_ref[...]
    columns = jnp.concatenate([dot(hi, place), dot(lo, place)], axis=1)
    owner = (iota((STATE, 2 * REQ_ROWS), 1) % REQ_ROWS) // 2
    per_chunk = 8
    for ch in range(REQ * LAYERS // per_chunk):
        span = range(ch * per_chunk, (ch + 1) * per_chunk)
        block = jnp.concatenate(
            [jnp.where(owner == m, columns, 0.0).astype(BF16) for m in span], axis=0
        )
        prod = dot(jnp.concatenate([states_ref[m] for m in span], axis=1), block)
        acc_buf[...] = prod if ch == 0 else acc_buf[...] + prod
    by_req = (acc_buf[:, 0:REQ_ROWS] + acc_buf[:, REQ_ROWS:]).T
    hi, mid, lo = split3(by_req)
    product_buf[...] = (dot(place, hi) + dot(place, mid) + dot(place, lo)).reshape(
        REPLICAS, ROWS, WIDTH
    )
    row, lane = iota((ROWS, 128), 0), iota((ROWS, 128), 1)
    mine = lane // 2 == row
    spread = one_hot(
        (iota((128, 128), 0) % 2 == iota((128, 128), 1) // HEAD_DIM) & (iota((128, 128), 0) < 16)
    )
    for t in range(TP):
        lanes = slice(t * RANK_WIDTH, (t + 1) * RANK_WIDTH)
        at = ROWS + (2 * t + 2) % ROWS
        tap2, tap3 = taps_ref[0, :, lanes][None], taps_ref[1, :, lanes][None]
        shift = params_ref[0, :, lanes][None]
        decay = params_ref[1, :, lanes][None]
        skip = params_ref[2, :, lanes][None]
        for q in range(0, REPLICAS, group):
            raw = got_ref[q : q + group, t, ROWS : 2 * ROWS, :].astype(F32)[
                :, at - ROWS : at - ROWS + 1, :
            ]
            raw = jnp.where(mine[None], raw, 0.0).astype(BF16).reshape(group * ROWS, 128)
            rate = dot(raw, spread).reshape(group, ROWS, 128) + shift
            dt = jnp.maximum(rate, 0.0) + jnp.log1p(jnp.exp(-jnp.abs(rate)))
            damp = jnp.exp(-dt * decay)
            fresh = got_ref[q : q + group, t, 0:ROWS, :].astype(F32)
            x = part_ref[q : q + group, :, lanes]
            x = x + tap2 * pltpu.roll(fresh, 1, 1) + tap3 * fresh
            x = x * jax.nn.sigmoid(x)
            taken = dt * x
            before = jnp.where(later, pltpu.roll(damp, 1, 1), 1.0)
            carried = jnp.where(later, pltpu.roll(taken, 1, 1) * dots_buf[1, q : q + group], 0.0)
            y = damp * (before * product_buf[q : q + group, :, lanes] + carried)
            y = y + taken * dots_buf[0, q : q + group] + skip * x
            out_ref[q : q + group, t] = y.astype(BF16)


def unpack_kernel(got_ref, out_ref):
    for r in range(N_REP):
        rows = jnp.concatenate([got_ref[r, h].astype(F32) for h in range(N_HEAD)], axis=1)
        for c in range(CAP):
            for l in range(LAYERS):
                at = (c * LAYERS + l) * STEPS
                out_ref[0, 0, r, c, l] = rows[at : at + STEPS].astype(BF16)


def shards(
    prefill_states,
    inner_tail,
    group_tail,
    assignment,
    decode_inner,
    decode_groups,
    decode_rate,
    conv_inner,
    conv_group,
    bias_inner,
    bias_group,
    rate_bias,
    decay_log,
    skip_gain,
):
    tail = (REQ, KERNEL - 1, LAYERS)
    packed, states, part, place, taps, params = pl.pallas_call(
        pack_kernel,
        out_shape=(
            jax.ShapeDtypeStruct((N_REP, N_HEAD, 2 * ROWS, 128), BF16),
            jax.ShapeDtypeStruct((REQ * LAYERS, WIDTH, STATE), BF16),
            jax.ShapeDtypeStruct((REPLICAS, ROWS, WIDTH + 2 * STATE), F32),
            jax.ShapeDtypeStruct((SLOT_ROWS, REQ_ROWS), BF16),
            jax.ShapeDtypeStruct((2, ROWS, WIDTH + 2 * STATE), F32),
            jax.ShapeDtypeStruct((3, ROWS, WIDTH), F32),
        ),
        in_specs=[HBM] * 14,
        out_specs=(VMEM,) * 6,
        scratch_shapes=[
            pltpu.VMEM(decode_inner.shape[2:], BF16),
            pltpu.VMEM((N_REP, STEPS, 2 * GROUP_SPAN), BF16),
            pltpu.VMEM(decode_rate.shape[2:], BF16),
            pltpu.VMEM((N_REP * ROWS, 2 * N_HEAD), F32),
            pltpu.VMEM((HIST_ROWS, WIDTH + 2 * STATE), F32),
            pltpu.VMEM(tail + (WIDTH,), BF16),
            pltpu.VMEM(tail + (STATE,), BF16),
            pltpu.VMEM(tail + (STATE,), BF16),
            pltpu.VMEM((1, REQ), jnp.int32),
            pltpu.VMEM((LAYERS, KERNEL, WIDTH), F32),
            pltpu.VMEM((LAYERS, KERNEL, STATE), F32),
            pltpu.VMEM((LAYERS, KERNEL, STATE), F32),
            pltpu.VMEM((LAYERS, WIDTH), F32),
            pltpu.VMEM((LAYERS, STATE), F32),
            pltpu.VMEM((LAYERS, STATE), F32),
            pltpu.VMEM((LAYERS, HEADS), F32),
            pltpu.VMEM((LAYERS, HEADS), F32),
            pltpu.VMEM((LAYERS, HEADS), F32),
            pltpu.SemaphoreType.DMA((17,)),
        ],
        compiler_params=pltpu.CompilerParams(vmem_limit_bytes=16 << 20),
        name="pack",
    )(
        *[
            pltpu.with_memory_space_constraint(v, pltpu.HBM)
            for v in (
                decode_inner,
                decode_groups,
                decode_rate,
                inner_tail.transpose(0, 2, 1, 3),
                group_tail.transpose(0, 2, 1, 3),
                assignment.reshape(1, REQ),
                conv_inner,
                conv_group,
                bias_inner,
                bias_group,
                rate_bias,
                decay_log,
                skip_gain,
                prefill_states.reshape(REQ * LAYERS, WIDTH, STATE),
            )
        ]
    )
    got = lax.all_to_all(
        packed.reshape(N_REP * N_HEAD, 2 * ROWS, 128), AXES, 0, 0, tiled=True
    ).reshape(REPLICAS, TP, 2 * ROWS, 128)
    decoded = pl.pallas_call(
        step_kernel,
        out_shape=jax.ShapeDtypeStruct((REPLICAS, TP, ROWS, 128), BF16),
        in_specs=[VMEM] * 6,
        out_specs=VMEM,
        scratch_shapes=[
            pltpu.VMEM((REPLICAS, ROWS, STATE), F32),
            pltpu.VMEM((2, REPLICAS, ROWS, 128), F32),
            pltpu.VMEM((WIDTH, 2 * REQ_ROWS), F32),
            pltpu.VMEM((REPLICAS, ROWS, WIDTH), F32),
        ],
        compiler_params=pltpu.CompilerParams(vmem_limit_bytes=16 << 20),
        name="step",
    )(got, states, part, place, taps, params)
    back = lax.all_to_all(
        decoded.reshape(REPLICAS * TP, ROWS, 128), AXES, 0, 0, tiled=True
    ).reshape(N_REP, N_HEAD, ROWS, 128)
    return pl.pallas_call(
        unpack_kernel,
        out_shape=jax.ShapeDtypeStruct((1, 1, N_REP, CAP, LAYERS, STEPS, N_HEAD * 128), BF16),
        in_specs=[VMEM],
        out_specs=VMEM,
        compiler_params=pltpu.CompilerParams(vmem_limit_bytes=16 << 20),
        name="unpack",
    )(back)


def solution(mesh):
    return jax.shard_map(
        shards,
        mesh=mesh,
        in_specs=(
            P("rep", None, "head", None, None),
            P("rep", None, None, "head"),
            P("rep", None, None, None),
            P("rep", None),
            P("rep", "head", None, None, None, None, None),
            P("rep", None, None, None, None, None, None),
            P("rep", "head", None, None, None, None, None),
            P(),
            P(),
            P(),
            P(),
            P(),
            P(),
            P(),
        ),
        out_specs=P("rep", "head", None, None, None, None, None),
        check_vma=False,
    )
```

```python
import jax
import jax.numpy as jnp
from jax import lax
from jax.experimental import pallas as pl
from jax.experimental.pallas import tpu as pltpu
from jax.sharding import PartitionSpec as P

F32 = jnp.float32
BF16 = jnp.bfloat16
AXES = ("rep", "head")
N_REP, N_HEAD, TP, CAP, LAYERS, STEPS, KERNEL = 8, 16, 4, 2, 2, 2, 4
SUBS = N_HEAD // TP
REPLICAS = N_REP * SUBS
REQ = 32
HEADS = 128
HEADS_LOCAL = HEADS // N_HEAD
HEAD_DIM, STATE = 64, 128
WIDTH = HEADS_LOCAL * HEAD_DIM
RANK_WIDTH = WIDTH // TP
GROUP_SPAN = 1024
ROWS = CAP * LAYERS * STEPS
SLOT_ROWS = REPLICAS * ROWS
HIST_ROWS = REQ * (KERNEL - 1) * LAYERS
VMEM = pl.BlockSpec(memory_space=pltpu.VMEM)
SMEM = pl.BlockSpec(memory_space=pltpu.SMEM)
HBM = pl.BlockSpec(memory_space=pltpu.HBM)


def iota(shape, dim):
    return lax.broadcasted_iota(jnp.int32, shape, dim)


def one_hot(cond):
    return jnp.where(cond, 1.0, 0.0).astype(BF16)


def dot(a, b):
    return jnp.dot(a, b, preferred_element_type=F32)


def split3(v):
    hi = v.astype(BF16)
    rest = v - hi.astype(F32)
    mid = rest.astype(BF16)
    return hi, mid, (rest - mid.astype(F32)).astype(BF16)


def pack_kernel(
    inner_hbm,
    group_hbm,
    rate_hbm,
    inner_tail_hbm,
    group_tail_hbm,
    chosen_hbm,
    conv_inner_hbm,
    conv_group_hbm,
    bias_inner_hbm,
    bias_group_hbm,
    rate_bias_hbm,
    decay_hbm,
    skip_hbm,
    states_hbm,
    out_ref,
    states_ref,
    slots_ref,
    part_ref,
    taps_ref,
    params_ref,
    inner_buf,
    group_buf,
    rate_ref,
    rate_buf,
    hist_buf,
    inner_tail_ref,
    tail_b_ref,
    tail_c_ref,
    chosen_ref,
    conv_inner_ref,
    conv_b_ref,
    conv_c_ref,
    bias_inner_ref,
    bias_b_ref,
    bias_c_ref,
    rate_bias_ref,
    decay_ref,
    skip_ref,
    listing,
    counts,
    sems,
):
    pos = lax.axis_index("head")
    sub, rank = lax.div(pos, TP), lax.rem(pos, TP)
    quarter = group_hbm.at[0, sub, :, lax.div(rank, LAYERS), lax.rem(rank, LAYERS)]
    copies = [
        pltpu.make_async_copy(src, dst, sems.at[13 + n])
        for n, (src, dst) in enumerate(
            ((rate_hbm.at[0, 0], rate_ref), (quarter, group_buf), (inner_hbm.at[0, 0], inner_buf))
        )
    ]
    for copy in copies:
        copy.start()
    inner = pl.ds(pl.multiple_of(pos * WIDTH, WIDTH), WIDTH)
    b = pl.ds(pl.multiple_of(lax.div(pos, 2) * STATE, STATE), STATE)
    c = pl.ds(pl.multiple_of(GROUP_SPAN + lax.div(pos, 2) * STATE, STATE), STATE)
    moves = (
        (chosen_hbm, chosen_ref),
        (inner_tail_hbm, inner_tail_ref),
        (group_tail_hbm.at[:, :, :, b], tail_b_ref),
        (group_tail_hbm.at[:, :, :, c], tail_c_ref),
        (conv_inner_hbm.at[:, :, inner], conv_inner_ref),
        (conv_group_hbm.at[:, :, b], conv_b_ref),
        (conv_group_hbm.at[:, :, c], conv_c_ref),
        (bias_inner_hbm.at[:, inner], bias_inner_ref),
        (bias_group_hbm.at[:, b], bias_b_ref),
        (bias_group_hbm.at[:, c], bias_c_ref),
        (rate_bias_hbm, rate_bias_ref),
        (decay_hbm, decay_ref),
        (skip_hbm, skip_ref),
    )
    tails = [pltpu.make_async_copy(src, dst, sems.at[n]) for n, (src, dst) in enumerate(moves)]
    for copy in tails:
        copy.start()
    near = pltpu.make_async_copy(states_hbm, states_ref, sems.at[16])
    near.start()
    listed = pltpu.make_async_copy(chosen_hbm, listing, sems.at[17])
    listed.start()
    for q in range(REPLICAS):
        counts[q] = 0
    turn = (iota((ROWS, 128), 0) - 2 * rank) & 7
    copies[0].wait()
    for r in range(N_REP):
        rate_buf[r * ROWS : (r + 1) * ROWS] = jnp.concatenate(
            [rate_ref[r, c, l].astype(F32) for c in range(CAP) for l in range(LAYERS)], axis=0
        )
    rates = rate_buf[...].astype(BF16)
    rate_rows = jnp.zeros((N_HEAD, N_REP * 128), F32)
    for u in range(2):
        pick = one_hot(iota((N_HEAD, 2 * N_HEAD), 1) == 2 * iota((N_HEAD, 2 * N_HEAD), 0) + u)
        turned = lax.dot_general(
            pick, rates, (((1,), (1,)), ((), ())), preferred_element_type=F32
        ).astype(BF16)
        shape = (N_REP * ROWS, N_REP * 128)
        row, lane = iota(shape, 0), iota(shape, 1)
        place = one_hot(
            (row // ROWS == lane // 128) & (lane % 128 == 2 * (row % ROWS) + u)
        )
        rate_rows = rate_rows + dot(turned, place)
    copies[1].wait()
    copies[2].wait()
    for r in range(N_REP):
        inner = jnp.concatenate(
            [inner_buf[r, c, l].astype(F32) for c in range(CAP) for l in range(LAYERS)], axis=0
        ).astype(BF16)
        fresh = group_buf[r].astype(F32)
        for h in range(N_HEAD):
            out_ref[r, h, 0:ROWS, :] = inner[:, h * 128 : (h + 1) * 128]
            at = (h // 2) * 128
            b_new = fresh[:, at : at + 128]
            c_new = fresh[:, GROUP_SPAN + at : GROUP_SPAN + at + 128]
            tile = jnp.where(turn == 0, b_new[0:1], 0.0)
            tile = jnp.where(turn == 1, b_new[1:2], tile)
            tile = jnp.where(turn == 4, c_new[0:1], tile)
            tile = jnp.where(turn == 5, c_new[1:2], tile)
            tile = jnp.where(turn == 2, rate_rows[h : h + 1, r * 128 : (r + 1) * 128], tile)
            out_ref[r, h, ROWS : 2 * ROWS, :] = tile.astype(BF16)
    for copy in tails:
        copy.wait()
    for i in range(REQ):
        for j in range(KERNEL - 1):
            rows = slice((i * 3 + j) * 2, (i * 3 + j) * 2 + 2)
            hist_buf[rows, 0:WIDTH] = inner_tail_ref[i, j].astype(F32)
            hist_buf[rows, WIDTH : WIDTH + STATE] = tail_b_ref[i, j].astype(F32)
            hist_buf[rows, WIDTH + STATE :] = tail_c_ref[i, j].astype(F32)
    listed.wait()
    for i in range(REQ):
        q = listing[0, i]
        rank = counts[q]
        slots_ref[i] = CAP * q + rank
        counts[q] = rank + 1
    chosen = chosen_ref[...].astype(F32)
    ri, ci = iota((REQ, REQ), 0), iota((REQ, REQ), 1)
    column = jnp.sum(jnp.where(ri == ci, chosen, 0.0), axis=1, keepdims=True)
    before = jnp.where((column == chosen) & (ri < ci), 1.0, 0.0)
    slots = CAP * chosen + jnp.sum(before, axis=0, keepdims=True)
    slots = jnp.broadcast_to(slots, (8, REQ)).astype(BF16)
    wide = dot(slots, one_hot(iota((REQ, HIST_ROWS), 1) // 6 == iota((REQ, HIST_ROWS), 0)))[0:1]
    col = iota((1, HIST_ROWS), 1)
    col_key = wide.astype(jnp.int32) * 8 + (col % 2) * 4 + (col % 6) // 2
    row = iota((SLOT_ROWS, HIST_ROWS), 0)
    row_key = (row // 4) * 8 + ((row // 2) % 2) * 4 + row % 2
    hist = hist_buf[...].astype(BF16)
    second = (iota((ROWS, 1), 0) // 2) % 2 == 1
    later = iota((ROWS, 1), 0) % 2 == 1

    def by_layer(first, other):
        return jnp.where(second, other, first)

    def weight(tap):
        rows = [ref[:, tap : tap + 1, :] for ref in (conv_inner_ref, conv_b_ref, conv_c_ref)]
        return jnp.concatenate([by_layer(w[0], w[1]) for w in rows], axis=1)

    offset = jnp.concatenate(
        [by_layer(ref[0:1], ref[1:2]) for ref in (bias_inner_ref, bias_b_ref, bias_c_ref)], axis=1
    )
    total = jnp.broadcast_to(offset[None], (REPLICAS, ROWS, WIDTH + 2 * STATE))
    for tap in range(KERNEL - 1):
        window = dot(one_hot(row_key + tap == col_key), hist)
        total = total + weight(tap)[None] * window.reshape(REPLICAS, ROWS, WIDTH + 2 * STATE)
    part_ref[...] = total
    taps_ref[0] = jnp.where(later, weight(2), 0.0)
    taps_ref[1] = weight(3)
    spread = one_hot(
        iota((HEADS, WIDTH), 0) == pos * HEADS_LOCAL + iota((HEADS, WIDTH), 1) // HEAD_DIM
    )
    for n, ref in enumerate((rate_bias_ref, decay_ref, skip_ref)):
        both = by_layer(ref[0:1], ref[1:2])
        hi, mid, lo = split3(both)
        value = dot(hi, spread) + dot(mid, spread) + dot(lo, spread)
        params_ref[n] = jnp.exp(value) if n == 1 else value
    near.wait()


def step_kernel(
    got_ref,
    states_ref,
    slots_ref,
    part_ref,
    taps_ref,
    params_ref,
    out_ref,
    read_buf,
    dots_buf,
    product_buf,
):
    pair = iota((1, ROWS, 128), 1) // 2
    later = iota((1, ROWS, 128), 1) % 2 == 1
    layer = (iota((1, 2 * ROWS, 128), 1) // STEPS) % LAYERS
    tap2_b = taps_ref[0, :, WIDTH : WIDTH + STATE][None]
    tap2_c = taps_ref[0, :, WIDTH + STATE :][None]
    tap3_b = taps_ref[1, :, WIDTH : WIDTH + STATE][None]
    tap3_c = taps_ref[1, :, WIDTH + STATE :][None]
    group = 4
    for q in range(0, REPLICAS, group):
        tiles = [got_ref[q : q + group, t, ROWS : 2 * ROWS, :].astype(F32) for t in range(TP)]
        b_new, c_new = tiles[0], tiles[2]
        for t in range(1, TP):
            b_new = jnp.where(pair == t, tiles[t], b_new)
            c_new = jnp.where(pair == t, tiles[(t + 2) % TP], c_new)
        c_new = pltpu.roll(c_new, 4, 1)
        b_act = part_ref[q : q + group, :, WIDTH : WIDTH + STATE]
        c_act = part_ref[q : q + group, :, WIDTH + STATE :]
        b_act = b_act + tap2_b * pltpu.roll(b_new, 1, 1) + tap3_b * b_new
        c_act = c_act + tap2_c * pltpu.roll(c_new, 1, 1) + tap3_c * c_new
        b_act = b_act * jax.nn.sigmoid(b_act)
        c_act = c_act * jax.nn.sigmoid(c_act)
        hi = c_act.astype(BF16).astype(F32)
        both = jnp.concatenate([hi, c_act - hi], axis=1)
        halves = [jnp.where(layer == l, both, 0.0) for l in range(LAYERS)]
        read_buf[q : q + group] = jnp.concatenate(halves, axis=2).astype(BF16)
        same = jnp.sum(b_act * c_act, axis=2, keepdims=True)
        cross = jnp.sum(pltpu.roll(b_act, 1, 1) * c_act, axis=2, keepdims=True)
        dots_buf[0, q : q + group] = jnp.broadcast_to(same, (group, ROWS, 128))
        dots_buf[1, q : q + group] = jnp.broadcast_to(cross, (group, ROWS, 128))
    product_buf[...] = jnp.zeros_like(product_buf)
    rank_of_row = iota((ROWS, WIDTH), 0) // (LAYERS * STEPS)
    for i in range(REQ):
        q, rank = lax.shift_right_logical(slots_ref[i], 1), slots_ref[i] & 1
        state = jnp.concatenate([states_ref[i * LAYERS + l] for l in range(LAYERS)], axis=1)
        prod = lax.dot_general(
            read_buf[q], state, (((1,), (1,)), ((), ())), preferred_element_type=F32
        )
        prod = prod[0:ROWS] + prod[ROWS:]
        product_buf[q] = product_buf[q] + jnp.where(rank_of_row == rank, prod, 0.0)
    row, lane = iota((ROWS, 128), 0), iota((ROWS, 128), 1)
    mine = lane // 2 == row
    spread = one_hot(
        (iota((128, 128), 0) % 2 == iota((128, 128), 1) // HEAD_DIM) & (iota((128, 128), 0) < 16)
    )
    for t in range(TP):
        lanes = slice(t * RANK_WIDTH, (t + 1) * RANK_WIDTH)
        at = ROWS + (2 * t + 2) % ROWS
        tap2, tap3 = taps_ref[0, :, lanes][None], taps_ref[1, :, lanes][None]
        shift = params_ref[0, :, lanes][None]
        decay = params_ref[1, :, lanes][None]
        skip = params_ref[2, :, lanes][None]
        for q in range(0, REPLICAS, group):
            raw = got_ref[q : q + group, t, ROWS : 2 * ROWS, :].astype(F32)[
                :, at - ROWS : at - ROWS + 1, :
            ]
            raw = jnp.where(mine[None], raw, 0.0).astype(BF16).reshape(group * ROWS, 128)
            rate = dot(raw, spread).reshape(group, ROWS, 128) + shift
            dt = jnp.maximum(rate, 0.0) + jnp.log1p(jnp.exp(-jnp.abs(rate)))
            damp = jnp.exp(-dt * decay)
            fresh = got_ref[q : q + group, t, 0:ROWS, :].astype(F32)
            x = part_ref[q : q + group, :, lanes]
            x = x + tap2 * pltpu.roll(fresh, 1, 1) + tap3 * fresh
            x = x * jax.nn.sigmoid(x)
            taken = dt * x
            before = jnp.where(later, pltpu.roll(damp, 1, 1), 1.0)
            carried = jnp.where(later, pltpu.roll(taken, 1, 1) * dots_buf[1, q : q + group], 0.0)
            y = damp * (before * product_buf[q : q + group, :, lanes] + carried)
            y = y + taken * dots_buf[0, q : q + group] + skip * x
            out_ref[q : q + group, t] = y.astype(BF16)


def unpack_kernel(got_ref, out_ref):
    for r in range(N_REP):
        rows = jnp.concatenate([got_ref[r, h].astype(F32) for h in range(N_HEAD)], axis=1)
        for c in range(CAP):
            for l in range(LAYERS):
                at = (c * LAYERS + l) * STEPS
                out_ref[0, 0, r, c, l] = rows[at : at + STEPS].astype(BF16)


def shards(
    prefill_states,
    inner_tail,
    group_tail,
    assignment,
    decode_inner,
    decode_groups,
    decode_rate,
    conv_inner,
    conv_group,
    bias_inner,
    bias_group,
    rate_bias,
    decay_log,
    skip_gain,
):
    states = pltpu.with_memory_space_constraint(
        prefill_states.reshape(REQ * LAYERS, WIDTH, STATE), pltpu.HBM
    )
    chosen = pltpu.with_memory_space_constraint(assignment.reshape(1, REQ), pltpu.HBM)
    tail = (REQ, KERNEL - 1, LAYERS)
    packed, near, slots, part, taps, params = pl.pallas_call(
        pack_kernel,
        out_shape=(
            jax.ShapeDtypeStruct((N_REP, N_HEAD, 2 * ROWS, 128), BF16),
            jax.ShapeDtypeStruct((REQ * LAYERS, WIDTH, STATE), BF16),
            pltpu.SMEM((REQ,), jnp.int32),
            jax.ShapeDtypeStruct((REPLICAS, ROWS, WIDTH + 2 * STATE), F32),
            jax.ShapeDtypeStruct((2, ROWS, WIDTH + 2 * STATE), F32),
            jax.ShapeDtypeStruct((3, ROWS, WIDTH), F32),
        ),
        in_specs=[HBM] * 14,
        out_specs=(VMEM, VMEM, SMEM, VMEM, VMEM, VMEM),
        scratch_shapes=[
            pltpu.VMEM(decode_inner.shape[2:], BF16),
            pltpu.VMEM((N_REP, STEPS, 2 * GROUP_SPAN), BF16),
            pltpu.VMEM(decode_rate.shape[2:], BF16),
            pltpu.VMEM((N_REP * ROWS, 2 * N_HEAD), F32),
            pltpu.VMEM((HIST_ROWS, WIDTH + 2 * STATE), F32),
            pltpu.VMEM(tail + (WIDTH,), BF16),
            pltpu.VMEM(tail + (STATE,), BF16),
            pltpu.VMEM(tail + (STATE,), BF16),
            pltpu.VMEM((1, REQ), jnp.int32),
            pltpu.VMEM((LAYERS, KERNEL, WIDTH), F32),
            pltpu.VMEM((LAYERS, KERNEL, STATE), F32),
            pltpu.VMEM((LAYERS, KERNEL, STATE), F32),
            pltpu.VMEM((LAYERS, WIDTH), F32),
            pltpu.VMEM((LAYERS, STATE), F32),
            pltpu.VMEM((LAYERS, STATE), F32),
            pltpu.VMEM((LAYERS, HEADS), F32),
            pltpu.VMEM((LAYERS, HEADS), F32),
            pltpu.VMEM((LAYERS, HEADS), F32),
            pltpu.SMEM((1, REQ), jnp.int32),
            pltpu.SMEM((REPLICAS,), jnp.int32),
            pltpu.SemaphoreType.DMA((18,)),
        ],
        compiler_params=pltpu.CompilerParams(vmem_limit_bytes=16 << 20),
        name="pack",
    )(
        *[
            pltpu.with_memory_space_constraint(v, pltpu.HBM)
            for v in (
                decode_inner,
                decode_groups,
                decode_rate,
                inner_tail.transpose(0, 2, 1, 3),
                group_tail.transpose(0, 2, 1, 3),
                chosen,
                conv_inner,
                conv_group,
                bias_inner,
                bias_group,
                rate_bias,
                decay_log,
                skip_gain,
                states,
            )
        ]
    )
    got = lax.all_to_all(
        packed.reshape(N_REP * N_HEAD, 2 * ROWS, 128), AXES, 0, 0, tiled=True
    ).reshape(REPLICAS, TP, 2 * ROWS, 128)
    decoded = pl.pallas_call(
        step_kernel,
        out_shape=jax.ShapeDtypeStruct((REPLICAS, TP, ROWS, 128), BF16),
        in_specs=[VMEM, VMEM, SMEM, VMEM, VMEM, VMEM],
        out_specs=VMEM,
        scratch_shapes=[
            pltpu.VMEM((REPLICAS, 2 * ROWS, LAYERS * STATE), BF16),
            pltpu.VMEM((2, REPLICAS, ROWS, 128), F32),
            pltpu.VMEM((REPLICAS, ROWS, WIDTH), F32),
        ],
        compiler_params=pltpu.CompilerParams(vmem_limit_bytes=20 << 20),
        name="step",
    )(got, near, slots, part, taps, params)
    back = lax.all_to_all(
        decoded.reshape(REPLICAS * TP, ROWS, 128), AXES, 0, 0, tiled=True
    ).reshape(N_REP, N_HEAD, ROWS, 128)
    return pl.pallas_call(
        unpack_kernel,
        out_shape=jax.ShapeDtypeStruct((1, 1, N_REP, CAP, LAYERS, STEPS, N_HEAD * 128), BF16),
        in_specs=[VMEM],
        out_specs=VMEM,
        compiler_params=pltpu.CompilerParams(vmem_limit_bytes=16 << 20),
        name="unpack",
    )(back)


def solution(mesh):
    return jax.shard_map(
        shards,
        mesh=mesh,
        in_specs=(
            P("rep", None, "head", None, None),
            P("rep", None, None, "head"),
            P("rep", None, None, None),
            P("rep", None),
            P("rep", "head", None, None, None, None, None),
            P("rep", None, None, None, None, None, None),
            P("rep", "head", None, None, None, None, None),
            P(),
            P(),
            P(),
            P(),
            P(),
            P(),
            P(),
        ),
        out_specs=P("rep", "head", None, None, None, None, None),
        check_vma=False,
    )
```

```python
import jax
import jax.numpy as jnp
from jax import lax
from jax.experimental import pallas as pl
from jax.experimental.pallas import tpu as pltpu
from jax.sharding import PartitionSpec as P

F32 = jnp.float32
BF16 = jnp.bfloat16
AXES = ("rep", "head")
N_REP, N_HEAD, TP, CAP, LAYERS, STEPS, KERNEL = 8, 16, 4, 2, 2, 2, 4
SUBS = N_HEAD // TP
REPLICAS = N_REP * SUBS
REQ = 32
HEADS = 128
HEADS_LOCAL = HEADS // N_HEAD
HEAD_DIM, STATE = 64, 128
WIDTH = HEADS_LOCAL * HEAD_DIM
RANK_WIDTH = WIDTH // TP
GROUP_SPAN = 1024
ROWS = CAP * LAYERS * STEPS
SLOT_ROWS = REPLICAS * ROWS
FAR = 14
NEAR = REQ - FAR
PIECE = 7
HIST_ROWS = REQ * (KERNEL - 1) * LAYERS
VMEM = pl.BlockSpec(memory_space=pltpu.VMEM)
SMEM = pl.BlockSpec(memory_space=pltpu.SMEM)
HBM = pl.BlockSpec(memory_space=pltpu.HBM)


def iota(shape, dim):
    return lax.broadcasted_iota(jnp.int32, shape, dim)


def one_hot(cond):
    return jnp.where(cond, 1.0, 0.0).astype(BF16)


def dot(a, b):
    return jnp.dot(a, b, preferred_element_type=F32)


def split3(v):
    hi = v.astype(BF16)
    rest = v - hi.astype(F32)
    mid = rest.astype(BF16)
    return hi, mid, (rest - mid.astype(F32)).astype(BF16)


def pack_kernel(
    inner_hbm,
    group_hbm,
    rate_hbm,
    inner_tail_hbm,
    group_tail_hbm,
    chosen_hbm,
    conv_inner_hbm,
    conv_group_hbm,
    bias_inner_hbm,
    bias_group_hbm,
    rate_bias_hbm,
    decay_hbm,
    skip_hbm,
    states_hbm,
    out_ref,
    states_ref,
    slots_ref,
    part_ref,
    taps_ref,
    params_ref,
    inner_buf,
    group_buf,
    rate_ref,
    rate_buf,
    hist_buf,
    inner_tail_ref,
    tail_b_ref,
    tail_c_ref,
    chosen_ref,
    conv_inner_ref,
    conv_b_ref,
    conv_c_ref,
    bias_inner_ref,
    bias_b_ref,
    bias_c_ref,
    rate_bias_ref,
    decay_ref,
    skip_ref,
    listing,
    counts,
    sems,
):
    pos = lax.axis_index("head")
    sub, rank = lax.div(pos, TP), lax.rem(pos, TP)
    quarter = group_hbm.at[0, sub, :, lax.div(rank, LAYERS), lax.rem(rank, LAYERS)]
    copies = [
        pltpu.make_async_copy(src, dst, sems.at[13 + n])
        for n, (src, dst) in enumerate(
            ((rate_hbm.at[0, 0], rate_ref), (quarter, group_buf), (inner_hbm.at[0, 0], inner_buf))
        )
    ]
    for copy in copies:
        copy.start()
    inner = pl.ds(pl.multiple_of(pos * WIDTH, WIDTH), WIDTH)
    b = pl.ds(pl.multiple_of(lax.div(pos, 2) * STATE, STATE), STATE)
    c = pl.ds(pl.multiple_of(GROUP_SPAN + lax.div(pos, 2) * STATE, STATE), STATE)
    moves = (
        (chosen_hbm, chosen_ref),
        (inner_tail_hbm, inner_tail_ref),
        (group_tail_hbm.at[:, :, :, b], tail_b_ref),
        (group_tail_hbm.at[:, :, :, c], tail_c_ref),
        (conv_inner_hbm.at[:, :, inner], conv_inner_ref),
        (conv_group_hbm.at[:, :, b], conv_b_ref),
        (conv_group_hbm.at[:, :, c], conv_c_ref),
        (bias_inner_hbm.at[:, inner], bias_inner_ref),
        (bias_group_hbm.at[:, b], bias_b_ref),
        (bias_group_hbm.at[:, c], bias_c_ref),
        (rate_bias_hbm, rate_bias_ref),
        (decay_hbm, decay_ref),
        (skip_hbm, skip_ref),
    )
    tails = [pltpu.make_async_copy(src, dst, sems.at[n]) for n, (src, dst) in enumerate(moves)]
    for copy in tails:
        copy.start()
    listed = pltpu.make_async_copy(chosen_hbm, listing, sems.at[17])
    listed.start()
    near = pltpu.make_async_copy(states_hbm.at[pl.ds(0, NEAR * LAYERS)], states_ref, sems.at[16])
    near.start()

    @pl.loop(0, REPLICAS)
    def _(q):
        counts[q] = 0

    turn = (iota((ROWS, 128), 0) - 2 * rank) & 7
    copies[0].wait()
    for r in range(N_REP):
        rate_buf[r * ROWS : (r + 1) * ROWS] = jnp.concatenate(
            [rate_ref[r, c, l].astype(F32) for c in range(CAP) for l in range(LAYERS)], axis=0
        )
    rates = rate_buf[...].astype(BF16)
    rate_rows = jnp.zeros((N_HEAD, N_REP * 128), F32)
    for u in range(2):
        pick = one_hot(iota((N_HEAD, 2 * N_HEAD), 1) == 2 * iota((N_HEAD, 2 * N_HEAD), 0) + u)
        turned = lax.dot_general(
            pick, rates, (((1,), (1,)), ((), ())), preferred_element_type=F32
        ).astype(BF16)
        shape = (N_REP * ROWS, N_REP * 128)
        row, lane = iota(shape, 0), iota(shape, 1)
        place = one_hot(
            (row // ROWS == lane // 128) & (lane % 128 == 2 * (row % ROWS) + u)
        )
        rate_rows = rate_rows + dot(turned, place)
    copies[1].wait()
    copies[2].wait()
    for r in range(N_REP):
        inner = jnp.concatenate(
            [inner_buf[r, c, l].astype(F32) for c in range(CAP) for l in range(LAYERS)], axis=0
        ).astype(BF16)
        fresh = group_buf[r].astype(F32)
        for h in range(N_HEAD):
            out_ref[r, h, 0:ROWS, :] = inner[:, h * 128 : (h + 1) * 128]
            at = (h // 2) * 128
            b_new = fresh[:, at : at + 128]
            c_new = fresh[:, GROUP_SPAN + at : GROUP_SPAN + at + 128]
            tile = jnp.where(turn == 0, b_new[0:1], 0.0)
            tile = jnp.where(turn == 1, b_new[1:2], tile)
            tile = jnp.where(turn == 4, c_new[0:1], tile)
            tile = jnp.where(turn == 5, c_new[1:2], tile)
            tile = jnp.where(turn == 2, rate_rows[h : h + 1, r * 128 : (r + 1) * 128], tile)
            out_ref[r, h, ROWS : 2 * ROWS, :] = tile.astype(BF16)
    for copy in tails:
        copy.wait()
    for i in range(REQ):
        for j in range(KERNEL - 1):
            rows = slice((i * 3 + j) * 2, (i * 3 + j) * 2 + 2)
            hist_buf[rows, 0:WIDTH] = inner_tail_ref[i, j].astype(F32)
            hist_buf[rows, WIDTH : WIDTH + STATE] = tail_b_ref[i, j].astype(F32)
            hist_buf[rows, WIDTH + STATE :] = tail_c_ref[i, j].astype(F32)
    listed.wait()
    for i in range(REQ):
        q = listing[0, i]
        rank = counts[q]
        slots_ref[i] = CAP * q + rank
        counts[q] = rank + 1
    chosen = chosen_ref[...].astype(F32)
    ri, ci = iota((REQ, REQ), 0), iota((REQ, REQ), 1)
    column = jnp.sum(jnp.where(ri == ci, chosen, 0.0), axis=1, keepdims=True)
    before = jnp.where((column == chosen) & (ri < ci), 1.0, 0.0)
    slots = CAP * chosen + jnp.sum(before, axis=0, keepdims=True)
    slots = jnp.broadcast_to(slots, (8, REQ)).astype(BF16)
    wide = dot(slots, one_hot(iota((REQ, HIST_ROWS), 1) // 6 == iota((REQ, HIST_ROWS), 0)))[0:1]
    col = iota((1, HIST_ROWS), 1)
    col_key = wide.astype(jnp.int32) * 8 + (col % 2) * 4 + (col % 6) // 2
    row = iota((SLOT_ROWS, HIST_ROWS), 0)
    row_key = (row // 4) * 8 + ((row // 2) % 2) * 4 + row % 2
    hist = hist_buf[...].astype(BF16)
    second = (iota((ROWS, 1), 0) // 2) % 2 == 1
    later = iota((ROWS, 1), 0) % 2 == 1

    def by_layer(first, other):
        return jnp.where(second, other, first)

    def weight(tap):
        rows = [ref[:, tap : tap + 1, :] for ref in (conv_inner_ref, conv_b_ref, conv_c_ref)]
        return jnp.concatenate([by_layer(w[0], w[1]) for w in rows], axis=1)

    offset = jnp.concatenate(
        [by_layer(ref[0:1], ref[1:2]) for ref in (bias_inner_ref, bias_b_ref, bias_c_ref)], axis=1
    )
    total = jnp.broadcast_to(offset[None], (REPLICAS, ROWS, WIDTH + 2 * STATE))
    for tap in range(KERNEL - 1):
        window = dot(one_hot(row_key + tap == col_key), hist)
        total = total + weight(tap)[None] * window.reshape(REPLICAS, ROWS, WIDTH + 2 * STATE)
    part_ref[...] = total
    taps_ref[0] = jnp.where(later, weight(2), 0.0)
    taps_ref[1] = weight(3)
    spread = one_hot(
        iota((HEADS, WIDTH), 0) == pos * HEADS_LOCAL + iota((HEADS, WIDTH), 1) // HEAD_DIM
    )
    for n, ref in enumerate((rate_bias_ref, decay_ref, skip_ref)):
        both = by_layer(ref[0:1], ref[1:2])
        hi, mid, lo = split3(both)
        value = dot(hi, spread) + dot(mid, spread) + dot(lo, spread)
        params_ref[n] = jnp.exp(value) if n == 1 else value
    near.wait()


def step_kernel(
    got_ref,
    near_ref,
    states_hbm,
    slots_ref,
    part_ref,
    taps_ref,
    params_ref,
    out_ref,
    read_buf,
    dots_buf,
    product_buf,
    base_buf,
    gain_buf,
    far_buf,
    sems,
):
    def fetch(n):
        return pltpu.make_async_copy(
            states_hbm.at[pl.ds((NEAR + n * PIECE) * LAYERS, PIECE * LAYERS)],
            far_buf.at[pl.ds(n * PIECE * LAYERS, PIECE * LAYERS)],
            sems.at[n],
        )

    @pl.loop(0, FAR // PIECE)
    def _(n):
        fetch(n).start()

    pair = iota((1, ROWS, 128), 1) // 2
    later = iota((1, ROWS, 128), 1) % 2 == 1
    layer = (iota((1, 2 * ROWS, 128), 1) // STEPS) % LAYERS
    tap2_b = taps_ref[0, :, WIDTH : WIDTH + STATE][None]
    tap2_c = taps_ref[0, :, WIDTH + STATE :][None]
    tap3_b = taps_ref[1, :, WIDTH : WIDTH + STATE][None]
    tap3_c = taps_ref[1, :, WIDTH + STATE :][None]
    group = 4
    for q in range(0, REPLICAS, group):
        tiles = [got_ref[q : q + group, t, ROWS : 2 * ROWS, :].astype(F32) for t in range(TP)]
        b_new, c_new = tiles[0], tiles[2]
        for t in range(1, TP):
            b_new = jnp.where(pair == t, tiles[t], b_new)
            c_new = jnp.where(pair == t, tiles[(t + 2) % TP], c_new)
        c_new = pltpu.roll(c_new, 4, 1)
        b_act = part_ref[q : q + group, :, WIDTH : WIDTH + STATE]
        c_act = part_ref[q : q + group, :, WIDTH + STATE :]
        b_act = b_act + tap2_b * pltpu.roll(b_new, 1, 1) + tap3_b * b_new
        c_act = c_act + tap2_c * pltpu.roll(c_new, 1, 1) + tap3_c * c_new
        b_act = b_act * jax.nn.sigmoid(b_act)
        c_act = c_act * jax.nn.sigmoid(c_act)
        hi = c_act.astype(BF16).astype(F32)
        both = jnp.concatenate([hi, c_act - hi], axis=1)
        halves = [jnp.where(layer == l, both, 0.0) for l in range(LAYERS)]
        read_buf[q : q + group] = jnp.concatenate(halves, axis=2).astype(BF16)
        same = jnp.sum(b_act * c_act, axis=2, keepdims=True)
        cross = jnp.sum(pltpu.roll(b_act, 1, 1) * c_act, axis=2, keepdims=True)
        dots_buf[0, q : q + group] = jnp.broadcast_to(same, (group, ROWS, 128))
        dots_buf[1, q : q + group] = jnp.broadcast_to(cross, (group, ROWS, 128))
    product_buf[...] = jnp.zeros_like(product_buf)
    row, lane = iota((ROWS, 128), 0), iota((ROWS, 128), 1)
    mine = lane // 2 == row
    spread = one_hot(
        (iota((128, 128), 0) % 2 == iota((128, 128), 1) // HEAD_DIM) & (iota((128, 128), 0) < 16)
    )

    def rest(t, q):
        lanes = slice(t * RANK_WIDTH, (t + 1) * RANK_WIDTH)
        at = (2 * t + 2) % ROWS
        tap2, tap3 = taps_ref[0, :, lanes][None], taps_ref[1, :, lanes][None]
        raw = got_ref[q : q + group, t, ROWS : 2 * ROWS, :].astype(F32)[:, at : at + 1, :]
        raw = jnp.where(mine[None], raw, 0.0).astype(BF16).reshape(group * ROWS, 128)
        rate = dot(raw, spread).reshape(group, ROWS, 128) + params_ref[0, :, lanes][None]
        dt = jnp.maximum(rate, 0.0) + jnp.log1p(jnp.exp(-jnp.abs(rate)))
        damp = jnp.exp(-dt * params_ref[1, :, lanes][None])
        fresh = got_ref[q : q + group, t, 0:ROWS, :].astype(F32)
        x = part_ref[q : q + group, :, lanes]
        x = x + tap2 * pltpu.roll(fresh, 1, 1) + tap3 * fresh
        x = x * jax.nn.sigmoid(x)
        taken = dt * x
        before = jnp.where(later, pltpu.roll(damp, 1, 1), 1.0)
        carried = jnp.where(later, pltpu.roll(taken, 1, 1) * dots_buf[1, q : q + group], 0.0)
        gain_buf[q : q + group, :, lanes] = damp * before
        base_buf[q : q + group, :, lanes] = (
            damp * carried + taken * dots_buf[0, q : q + group] + params_ref[2, :, lanes][None] * x
        )

    parts = [(t, q) for q in range(0, REPLICAS, group) for t in range(TP)]
    rank_of_row = iota((ROWS, WIDTH), 0) // (LAYERS * STEPS)
    for i in range(REQ):
        q, rank = lax.shift_right_logical(slots_ref[i], 1), slots_ref[i] & 1
        if i >= NEAR and (i - NEAR) % PIECE == 0:
            fetch((i - NEAR) // PIECE).wait()
        state = near_ref if i < NEAR else far_buf
        at = (i if i < NEAR else i - NEAR) * LAYERS
        state = jnp.concatenate([state[at + l] for l in range(LAYERS)], axis=1)
        prod = lax.dot_general(
            read_buf[q], state, (((1,), (1,)), ((), ())), preferred_element_type=F32
        )
        prod = prod[0:ROWS] + prod[ROWS:]
        product_buf[q] = product_buf[q] + jnp.where(rank_of_row == rank, prod, 0.0)
        rest(*parts[i])
    for q in range(0, REPLICAS, group):
        for t in range(TP):
            lanes = slice(t * RANK_WIDTH, (t + 1) * RANK_WIDTH)
            y = base_buf[q : q + group, :, lanes]
            y = y + gain_buf[q : q + group, :, lanes] * product_buf[q : q + group, :, lanes]
            out_ref[q : q + group, t] = y.astype(BF16)


def unpack_kernel(got_ref, out_ref):
    for r in range(N_REP):
        rows = jnp.concatenate([got_ref[r, h].astype(F32) for h in range(N_HEAD)], axis=1)
        for c in range(CAP):
            for l in range(LAYERS):
                at = (c * LAYERS + l) * STEPS
                out_ref[0, 0, r, c, l] = rows[at : at + STEPS].astype(BF16)


def shards(
    prefill_states,
    inner_tail,
    group_tail,
    assignment,
    decode_inner,
    decode_groups,
    decode_rate,
    conv_inner,
    conv_group,
    bias_inner,
    bias_group,
    rate_bias,
    decay_log,
    skip_gain,
):
    states = pltpu.with_memory_space_constraint(
        prefill_states.reshape(REQ * LAYERS, WIDTH, STATE), pltpu.HBM
    )
    chosen = pltpu.with_memory_space_constraint(assignment.reshape(1, REQ), pltpu.HBM)
    tail = (REQ, KERNEL - 1, LAYERS)
    packed, near, slots, part, taps, params = pl.pallas_call(
        pack_kernel,
        out_shape=(
            jax.ShapeDtypeStruct((N_REP, N_HEAD, 2 * ROWS, 128), BF16),
            jax.ShapeDtypeStruct((NEAR * LAYERS, WIDTH, STATE), BF16),
            pltpu.SMEM((REQ,), jnp.int32),
            jax.ShapeDtypeStruct((REPLICAS, ROWS, WIDTH + 2 * STATE), F32),
            jax.ShapeDtypeStruct((2, ROWS, WIDTH + 2 * STATE), F32),
            jax.ShapeDtypeStruct((3, ROWS, WIDTH), F32),
        ),
        in_specs=[HBM] * 14,
        out_specs=(VMEM, VMEM, SMEM, VMEM, VMEM, VMEM),
        scratch_shapes=[
            pltpu.VMEM(decode_inner.shape[2:], BF16),
            pltpu.VMEM((N_REP, STEPS, 2 * GROUP_SPAN), BF16),
            pltpu.VMEM(decode_rate.shape[2:], BF16),
            pltpu.VMEM((N_REP * ROWS, 2 * N_HEAD), F32),
            pltpu.VMEM((HIST_ROWS, WIDTH + 2 * STATE), F32),
            pltpu.VMEM(tail + (WIDTH,), BF16),
            pltpu.VMEM(tail + (STATE,), BF16),
            pltpu.VMEM(tail + (STATE,), BF16),
            pltpu.VMEM((1, REQ), jnp.int32),
            pltpu.VMEM((LAYERS, KERNEL, WIDTH), F32),
            pltpu.VMEM((LAYERS, KERNEL, STATE), F32),
            pltpu.VMEM((LAYERS, KERNEL, STATE), F32),
            pltpu.VMEM((LAYERS, WIDTH), F32),
            pltpu.VMEM((LAYERS, STATE), F32),
            pltpu.VMEM((LAYERS, STATE), F32),
            pltpu.VMEM((LAYERS, HEADS), F32),
            pltpu.VMEM((LAYERS, HEADS), F32),
            pltpu.VMEM((LAYERS, HEADS), F32),
            pltpu.SMEM((1, REQ), jnp.int32),
            pltpu.SMEM((REPLICAS,), jnp.int32),
            pltpu.SemaphoreType.DMA((18,)),
        ],
        compiler_params=pltpu.CompilerParams(vmem_limit_bytes=16 << 20),
        name="pack",
    )(
        *[
            pltpu.with_memory_space_constraint(v, pltpu.HBM)
            for v in (
                decode_inner,
                decode_groups,
                decode_rate,
                inner_tail.transpose(0, 2, 1, 3),
                group_tail.transpose(0, 2, 1, 3),
                chosen,
                conv_inner,
                conv_group,
                bias_inner,
                bias_group,
                rate_bias,
                decay_log,
                skip_gain,
                states,
            )
        ]
    )
    got = lax.all_to_all(
        packed.reshape(N_REP * N_HEAD, 2 * ROWS, 128), AXES, 0, 0, tiled=True
    ).reshape(REPLICAS, TP, 2 * ROWS, 128)
    decoded = pl.pallas_call(
        step_kernel,
        out_shape=jax.ShapeDtypeStruct((REPLICAS, TP, ROWS, 128), BF16),
        in_specs=[VMEM, VMEM, HBM, SMEM, VMEM, VMEM, VMEM],
        out_specs=VMEM,
        scratch_shapes=[
            pltpu.VMEM((REPLICAS, 2 * ROWS, LAYERS * STATE), BF16),
            pltpu.VMEM((2, REPLICAS, ROWS, 128), F32),
            pltpu.VMEM((REPLICAS, ROWS, WIDTH), F32),
            pltpu.VMEM((REPLICAS, ROWS, WIDTH), F32),
            pltpu.VMEM((REPLICAS, ROWS, WIDTH), F32),
            pltpu.VMEM((max(FAR, 1) * LAYERS, WIDTH, STATE), BF16),
            pltpu.SemaphoreType.DMA((FAR // PIECE,)),
        ],
        compiler_params=pltpu.CompilerParams(vmem_limit_bytes=20 << 20),
        name="step",
    )(got, near, states, slots, part, taps, params)
    back = lax.all_to_all(
        decoded.reshape(REPLICAS * TP, ROWS, 128), AXES, 0, 0, tiled=True
    ).reshape(N_REP, N_HEAD, ROWS, 128)
    return pl.pallas_call(
        unpack_kernel,
        out_shape=jax.ShapeDtypeStruct((1, 1, N_REP, CAP, LAYERS, STEPS, N_HEAD * 128), BF16),
        in_specs=[VMEM],
        out_specs=VMEM,
        compiler_params=pltpu.CompilerParams(vmem_limit_bytes=16 << 20),
        name="unpack",
    )(back)


def solution(mesh):
    return jax.shard_map(
        shards,
        mesh=mesh,
        in_specs=(
            P("rep", None, "head", None, None),
            P("rep", None, None, "head"),
            P("rep", None, None, None),
            P("rep", None),
            P("rep", "head", None, None, None, None, None),
            P("rep", None, None, None, None, None, None),
            P("rep", "head", None, None, None, None, None),
            P(),
            P(),
            P(),
            P(),
            P(),
            P(),
            P(),
        ),
        out_specs=P("rep", "head", None, None, None, None, None),
        check_vma=False,
    )
```

```python
import jax
import jax.numpy as jnp
from jax import lax
from jax.experimental import pallas as pl
from jax.experimental.pallas import tpu as pltpu
from jax.sharding import PartitionSpec as P

F32 = jnp.float32
BF16 = jnp.bfloat16
AXES = ("rep", "head")
N_REP, N_HEAD, TP, CAP, LAYERS, STEPS, KERNEL = 8, 16, 4, 2, 2, 2, 4
SUBS = N_HEAD // TP
REPLICAS = N_REP * SUBS
REQ = 32
HEADS = 128
HEADS_LOCAL = HEADS // N_HEAD
HEAD_DIM, STATE = 64, 128
WIDTH = HEADS_LOCAL * HEAD_DIM
RANK_WIDTH = WIDTH // TP
GROUP_SPAN = 1024
ROWS = CAP * LAYERS * STEPS
PAIRS = CAP * LAYERS + 3
SLOT_ROWS = REPLICAS * ROWS
FAR = 14
NEAR = REQ - FAR
PIECE = 7
HIST_ROWS = REQ * (KERNEL - 1) * LAYERS
VMEM = pl.BlockSpec(memory_space=pltpu.VMEM)
SMEM = pl.BlockSpec(memory_space=pltpu.SMEM)
HBM = pl.BlockSpec(memory_space=pltpu.HBM)


def iota(shape, dim):
    return lax.broadcasted_iota(jnp.int32, shape, dim)


def one_hot(cond):
    return jnp.where(cond, 1.0, 0.0).astype(BF16)


def dot(a, b):
    return jnp.dot(a, b, preferred_element_type=F32)


def split3(v):
    hi = v.astype(BF16)
    rest = v - hi.astype(F32)
    mid = rest.astype(BF16)
    return hi, mid, (rest - mid.astype(F32)).astype(BF16)


def pack_kernel(
    inner_hbm,
    group_hbm,
    rate_hbm,
    inner_tail_hbm,
    group_tail_hbm,
    chosen_hbm,
    conv_inner_hbm,
    conv_group_hbm,
    bias_inner_hbm,
    bias_group_hbm,
    rate_bias_hbm,
    decay_hbm,
    skip_hbm,
    states_hbm,
    out_ref,
    states_ref,
    slots_ref,
    part_ref,
    taps_ref,
    params_ref,
    inner_buf,
    group_buf,
    rate_ref,
    rate_buf,
    hist_buf,
    inner_tail_ref,
    tail_b_ref,
    tail_c_ref,
    chosen_ref,
    conv_inner_ref,
    conv_b_ref,
    conv_c_ref,
    bias_inner_ref,
    bias_b_ref,
    bias_c_ref,
    rate_bias_ref,
    decay_ref,
    skip_ref,
    listing,
    counts,
    sems,
):
    pos = lax.axis_index("head")
    sub, rank = lax.div(pos, TP), lax.rem(pos, TP)
    quarter = group_hbm.at[0, sub, :, lax.div(rank, LAYERS), lax.rem(rank, LAYERS)]
    copies = [
        pltpu.make_async_copy(src, dst, sems.at[13 + n])
        for n, (src, dst) in enumerate(
            ((rate_hbm.at[0, 0], rate_ref), (quarter, group_buf), (inner_hbm.at[0, 0], inner_buf))
        )
    ]
    for copy in copies:
        copy.start()
    inner = pl.ds(pl.multiple_of(pos * WIDTH, WIDTH), WIDTH)
    b = pl.ds(pl.multiple_of(lax.div(pos, 2) * STATE, STATE), STATE)
    c = pl.ds(pl.multiple_of(GROUP_SPAN + lax.div(pos, 2) * STATE, STATE), STATE)
    moves = (
        (chosen_hbm, chosen_ref),
        (inner_tail_hbm, inner_tail_ref),
        (group_tail_hbm.at[:, :, :, b], tail_b_ref),
        (group_tail_hbm.at[:, :, :, c], tail_c_ref),
        (conv_inner_hbm.at[:, :, inner], conv_inner_ref),
        (conv_group_hbm.at[:, :, b], conv_b_ref),
        (conv_group_hbm.at[:, :, c], conv_c_ref),
        (bias_inner_hbm.at[:, inner], bias_inner_ref),
        (bias_group_hbm.at[:, b], bias_b_ref),
        (bias_group_hbm.at[:, c], bias_c_ref),
        (rate_bias_hbm, rate_bias_ref),
        (decay_hbm, decay_ref),
        (skip_hbm, skip_ref),
    )
    tails = [pltpu.make_async_copy(src, dst, sems.at[n]) for n, (src, dst) in enumerate(moves)]
    for copy in tails:
        copy.start()
    listed = pltpu.make_async_copy(chosen_hbm, listing, sems.at[17])
    listed.start()
    near = pltpu.make_async_copy(states_hbm.at[pl.ds(0, NEAR * LAYERS)], states_ref, sems.at[16])
    near.start()

    @pl.loop(0, REPLICAS)
    def _(q):
        counts[q] = 0

    copies[0].wait()
    for r in range(N_REP):
        rate_buf[r * ROWS : (r + 1) * ROWS] = jnp.concatenate(
            [rate_ref[r, c, l].astype(F32) for c in range(CAP) for l in range(LAYERS)], axis=0
        )
    rates = rate_buf[...].astype(BF16)
    rate_rows = jnp.zeros((N_HEAD, N_REP * 128), F32)
    for u in range(2):
        pick = one_hot(iota((N_HEAD, 2 * N_HEAD), 1) == 2 * iota((N_HEAD, 2 * N_HEAD), 0) + u)
        turned = lax.dot_general(
            pick, rates, (((1,), (1,)), ((), ())), preferred_element_type=F32
        ).astype(BF16)
        shape = (N_REP * ROWS, N_REP * 128)
        row, lane = iota(shape, 0), iota(shape, 1)
        place = one_hot(
            (row // ROWS == lane // 128) & (lane % 128 == 2 * (row % ROWS) + u)
        )
        rate_rows = rate_rows + dot(turned, place)
    copies[1].wait()
    copies[2].wait()
    for r in range(N_REP):
        fresh = group_buf[r]
        inner = [inner_buf[r, c, l] for c in range(CAP) for l in range(LAYERS)]
        for h in range(N_HEAD):
            for m in range(CAP * LAYERS):
                out_ref[r, h, m] = inner[m][:, h * 128 : (h + 1) * 128]
            at = (h // 2) * 128
            out_ref[r, h, 4] = fresh[:, at : at + 128]
            out_ref[r, h, 5] = fresh[:, GROUP_SPAN + at : GROUP_SPAN + at + 128]
            out_ref[r, h, 6] = jnp.broadcast_to(
                rate_rows[h : h + 1, r * 128 : (r + 1) * 128], (2, 128)
            ).astype(BF16)
    for copy in tails:
        copy.wait()
    for i in range(REQ):
        for j in range(KERNEL - 1):
            rows = slice((i * 3 + j) * 2, (i * 3 + j) * 2 + 2)
            hist_buf[rows, 0:WIDTH] = inner_tail_ref[i, j].astype(F32)
            hist_buf[rows, WIDTH : WIDTH + STATE] = tail_b_ref[i, j].astype(F32)
            hist_buf[rows, WIDTH + STATE :] = tail_c_ref[i, j].astype(F32)
    listed.wait()
    for i in range(REQ):
        q = listing[0, i]
        rank = counts[q]
        slots_ref[i] = CAP * q + rank
        counts[q] = rank + 1
    chosen = chosen_ref[...].astype(F32)
    ri, ci = iota((REQ, REQ), 0), iota((REQ, REQ), 1)
    column = jnp.sum(jnp.where(ri == ci, chosen, 0.0), axis=1, keepdims=True)
    before = jnp.where((column == chosen) & (ri < ci), 1.0, 0.0)
    slots = CAP * chosen + jnp.sum(before, axis=0, keepdims=True)
    slots = jnp.broadcast_to(slots, (8, REQ)).astype(BF16)
    wide = dot(slots, one_hot(iota((REQ, HIST_ROWS), 1) // 6 == iota((REQ, HIST_ROWS), 0)))[0:1]
    col = iota((1, HIST_ROWS), 1)
    col_key = wide.astype(jnp.int32) * 8 + (col % 2) * 4 + (col % 6) // 2
    row = iota((SLOT_ROWS, HIST_ROWS), 0)
    row_key = (row // 4) * 8 + ((row // 2) % 2) * 4 + row % 2
    hist = hist_buf[...].astype(BF16)
    second = (iota((ROWS, 1), 0) // 2) % 2 == 1
    later = iota((ROWS, 1), 0) % 2 == 1

    def by_layer(first, other):
        return jnp.where(second, other, first)

    def weight(tap):
        rows = [ref[:, tap : tap + 1, :] for ref in (conv_inner_ref, conv_b_ref, conv_c_ref)]
        return jnp.concatenate([by_layer(w[0], w[1]) for w in rows], axis=1)

    offset = jnp.concatenate(
        [by_layer(ref[0:1], ref[1:2]) for ref in (bias_inner_ref, bias_b_ref, bias_c_ref)], axis=1
    )
    total = jnp.broadcast_to(offset[None], (REPLICAS, ROWS, WIDTH + 2 * STATE))
    for tap in range(KERNEL - 1):
        window = dot(one_hot(row_key + tap == col_key), hist)
        total = total + weight(tap)[None] * window.reshape(REPLICAS, ROWS, WIDTH + 2 * STATE)
    part_ref[...] = total
    taps_ref[0] = jnp.where(later, weight(2), 0.0)
    taps_ref[1] = weight(3)
    spread = one_hot(
        iota((HEADS, WIDTH), 0) == pos * HEADS_LOCAL + iota((HEADS, WIDTH), 1) // HEAD_DIM
    )
    for n, ref in enumerate((rate_bias_ref, decay_ref, skip_ref)):
        both = by_layer(ref[0:1], ref[1:2])
        hi, mid, lo = split3(both)
        value = dot(hi, spread) + dot(mid, spread) + dot(lo, spread)
        params_ref[n] = jnp.exp(value) if n == 1 else value
    near.wait()


def step_kernel(
    got_ref,
    near_ref,
    states_hbm,
    slots_ref,
    part_ref,
    taps_ref,
    params_ref,
    out_ref,
    read_buf,
    dots_buf,
    product_buf,
    base_buf,
    gain_buf,
    far_buf,
    sems,
):
    def fetch(n):
        return pltpu.make_async_copy(
            states_hbm.at[pl.ds((NEAR + n * PIECE) * LAYERS, PIECE * LAYERS)],
            far_buf.at[pl.ds(n * PIECE * LAYERS, PIECE * LAYERS)],
            sems.at[n],
        )

    @pl.loop(0, FAR // PIECE)
    def _(n):
        fetch(n).start()

    later = iota((1, ROWS, 128), 1) % 2 == 1
    layer = (iota((1, 2 * ROWS, 128), 1) // STEPS) % LAYERS
    tap2_b = taps_ref[0, :, WIDTH : WIDTH + STATE][None]
    tap2_c = taps_ref[0, :, WIDTH + STATE :][None]
    tap3_b = taps_ref[1, :, WIDTH : WIDTH + STATE][None]
    tap3_c = taps_ref[1, :, WIDTH + STATE :][None]
    group = 4
    for q in range(0, REPLICAS, group):
        b_new, c_new = [
            jnp.concatenate([got_ref[q : q + group, t, m].astype(F32) for t in range(TP)], axis=1)
            for m in (4, 5)
        ]
        b_act = part_ref[q : q + group, :, WIDTH : WIDTH + STATE]
        c_act = part_ref[q : q + group, :, WIDTH + STATE :]
        b_act = b_act + tap2_b * pltpu.roll(b_new, 1, 1) + tap3_b * b_new
        c_act = c_act + tap2_c * pltpu.roll(c_new, 1, 1) + tap3_c * c_new
        b_act = b_act * jax.nn.sigmoid(b_act)
        c_act = c_act * jax.nn.sigmoid(c_act)
        hi = c_act.astype(BF16).astype(F32)
        both = jnp.concatenate([hi, c_act - hi], axis=1)
        halves = [jnp.where(layer == l, both, 0.0) for l in range(LAYERS)]
        read_buf[q : q + group] = jnp.concatenate(halves, axis=2).astype(BF16)
        same = jnp.sum(b_act * c_act, axis=2, keepdims=True)
        cross = jnp.sum(pltpu.roll(b_act, 1, 1) * c_act, axis=2, keepdims=True)
        dots_buf[0, q : q + group] = jnp.broadcast_to(same, (group, ROWS, 128))
        dots_buf[1, q : q + group] = jnp.broadcast_to(cross, (group, ROWS, 128))
    product_buf[...] = jnp.zeros_like(product_buf)
    row, lane = iota((ROWS, 128), 0), iota((ROWS, 128), 1)
    mine = lane // 2 == row
    spread = one_hot(
        (iota((128, 128), 0) % 2 == iota((128, 128), 1) // HEAD_DIM) & (iota((128, 128), 0) < 16)
    )

    def rest(t, q):
        lanes = slice(t * RANK_WIDTH, (t + 1) * RANK_WIDTH)
        tap2, tap3 = taps_ref[0, :, lanes][None], taps_ref[1, :, lanes][None]
        raw = got_ref[q : q + group, t, 6].astype(F32)[:, 0:1, :]
        raw = jnp.where(mine[None], raw, 0.0).astype(BF16).reshape(group * ROWS, 128)
        rate = dot(raw, spread).reshape(group, ROWS, 128) + params_ref[0, :, lanes][None]
        dt = jnp.maximum(rate, 0.0) + jnp.log1p(jnp.exp(-jnp.abs(rate)))
        damp = jnp.exp(-dt * params_ref[1, :, lanes][None])
        fresh = jnp.concatenate(
            [got_ref[q : q + group, t, m].astype(F32) for m in range(CAP * LAYERS)], axis=1
        )
        x = part_ref[q : q + group, :, lanes]
        x = x + tap2 * pltpu.roll(fresh, 1, 1) + tap3 * fresh
        x = x * jax.nn.sigmoid(x)
        taken = dt * x
        before = jnp.where(later, pltpu.roll(damp, 1, 1), 1.0)
        carried = jnp.where(later, pltpu.roll(taken, 1, 1) * dots_buf[1, q : q + group], 0.0)
        gain_buf[q : q + group, :, lanes] = damp * before
        base_buf[q : q + group, :, lanes] = (
            damp * carried + taken * dots_buf[0, q : q + group] + params_ref[2, :, lanes][None] * x
        )

    parts = [(t, q) for q in range(0, REPLICAS, group) for t in range(TP)]
    rank_of_row = iota((ROWS, WIDTH), 0) // (LAYERS * STEPS)
    for i in range(REQ):
        q, rank = lax.shift_right_logical(slots_ref[i], 1), slots_ref[i] & 1
        if i >= NEAR and (i - NEAR) % PIECE == 0:
            fetch((i - NEAR) // PIECE).wait()
        state = near_ref if i < NEAR else far_buf
        at = (i if i < NEAR else i - NEAR) * LAYERS
        state = jnp.concatenate([state[at + l] for l in range(LAYERS)], axis=1)
        prod = lax.dot_general(
            read_buf[q], state, (((1,), (1,)), ((), ())), preferred_element_type=F32
        )
        prod = prod[0:ROWS] + prod[ROWS:]
        product_buf[q] = product_buf[q] + jnp.where(rank_of_row == rank, prod, 0.0)
        rest(*parts[i])
    for q in range(0, REPLICAS, group):
        for t in range(TP):
            lanes = slice(t * RANK_WIDTH, (t + 1) * RANK_WIDTH)
            y = base_buf[q : q + group, :, lanes]
            y = y + gain_buf[q : q + group, :, lanes] * product_buf[q : q + group, :, lanes]
            out_ref[q : q + group, t] = y.astype(BF16)


def unpack_kernel(got_ref, out_ref):
    for r in range(N_REP):
        rows = jnp.concatenate([got_ref[r, h].astype(F32) for h in range(N_HEAD)], axis=1)
        for c in range(CAP):
            for l in range(LAYERS):
                at = (c * LAYERS + l) * STEPS
                out_ref[0, 0, r, c, l] = rows[at : at + STEPS].astype(BF16)


def shards(
    prefill_states,
    inner_tail,
    group_tail,
    assignment,
    decode_inner,
    decode_groups,
    decode_rate,
    conv_inner,
    conv_group,
    bias_inner,
    bias_group,
    rate_bias,
    decay_log,
    skip_gain,
):
    states = pltpu.with_memory_space_constraint(
        prefill_states.reshape(REQ * LAYERS, WIDTH, STATE), pltpu.HBM
    )
    chosen = pltpu.with_memory_space_constraint(assignment.reshape(1, REQ), pltpu.HBM)
    tail = (REQ, KERNEL - 1, LAYERS)
    packed, near, slots, part, taps, params = pl.pallas_call(
        pack_kernel,
        out_shape=(
            jax.ShapeDtypeStruct((N_REP, N_HEAD, PAIRS, 2, 128), BF16),
            jax.ShapeDtypeStruct((NEAR * LAYERS, WIDTH, STATE), BF16),
            pltpu.SMEM((REQ,), jnp.int32),
            jax.ShapeDtypeStruct((REPLICAS, ROWS, WIDTH + 2 * STATE), F32),
            jax.ShapeDtypeStruct((2, ROWS, WIDTH + 2 * STATE), F32),
            jax.ShapeDtypeStruct((3, ROWS, WIDTH), F32),
        ),
        in_specs=[HBM] * 14,
        out_specs=(VMEM, VMEM, SMEM, VMEM, VMEM, VMEM),
        scratch_shapes=[
            pltpu.VMEM(decode_inner.shape[2:], BF16),
            pltpu.VMEM((N_REP, STEPS, 2 * GROUP_SPAN), BF16),
            pltpu.VMEM(decode_rate.shape[2:], BF16),
            pltpu.VMEM((N_REP * ROWS, 2 * N_HEAD), F32),
            pltpu.VMEM((HIST_ROWS, WIDTH + 2 * STATE), F32),
            pltpu.VMEM(tail + (WIDTH,), BF16),
            pltpu.VMEM(tail + (STATE,), BF16),
            pltpu.VMEM(tail + (STATE,), BF16),
            pltpu.VMEM((1, REQ), jnp.int32),
            pltpu.VMEM((LAYERS, KERNEL, WIDTH), F32),
            pltpu.VMEM((LAYERS, KERNEL, STATE), F32),
            pltpu.VMEM((LAYERS, KERNEL, STATE), F32),
            pltpu.VMEM((LAYERS, WIDTH), F32),
            pltpu.VMEM((LAYERS, STATE), F32),
            pltpu.VMEM((LAYERS, STATE), F32),
            pltpu.VMEM((LAYERS, HEADS), F32),
            pltpu.VMEM((LAYERS, HEADS), F32),
            pltpu.VMEM((LAYERS, HEADS), F32),
            pltpu.SMEM((1, REQ), jnp.int32),
            pltpu.SMEM((REPLICAS,), jnp.int32),
            pltpu.SemaphoreType.DMA((18,)),
        ],
        compiler_params=pltpu.CompilerParams(vmem_limit_bytes=16 << 20),
        name="pack",
    )(
        *[
            pltpu.with_memory_space_constraint(v, pltpu.HBM)
            for v in (
                decode_inner,
                decode_groups,
                decode_rate,
                inner_tail.transpose(0, 2, 1, 3),
                group_tail.transpose(0, 2, 1, 3),
                chosen,
                conv_inner,
                conv_group,
                bias_inner,
                bias_group,
                rate_bias,
                decay_log,
                skip_gain,
                states,
            )
        ]
    )
    got = lax.all_to_all(
        packed.reshape(N_REP * N_HEAD, PAIRS, 2, 128), AXES, 0, 0, tiled=True
    ).reshape(REPLICAS, TP, PAIRS, 2, 128)
    decoded = pl.pallas_call(
        step_kernel,
        out_shape=jax.ShapeDtypeStruct((REPLICAS, TP, ROWS, 128), BF16),
        in_specs=[VMEM, VMEM, HBM, SMEM, VMEM, VMEM, VMEM],
        out_specs=VMEM,
        scratch_shapes=[
            pltpu.VMEM((REPLICAS, 2 * ROWS, LAYERS * STATE), BF16),
            pltpu.VMEM((2, REPLICAS, ROWS, 128), F32),
            pltpu.VMEM((REPLICAS, ROWS, WIDTH), F32),
            pltpu.VMEM((REPLICAS, ROWS, WIDTH), F32),
            pltpu.VMEM((REPLICAS, ROWS, WIDTH), F32),
            pltpu.VMEM((max(FAR, 1) * LAYERS, WIDTH, STATE), BF16),
            pltpu.SemaphoreType.DMA((FAR // PIECE,)),
        ],
        compiler_params=pltpu.CompilerParams(vmem_limit_bytes=20 << 20),
        name="step",
    )(got, near, states, slots, part, taps, params)
    back = lax.all_to_all(
        decoded.reshape(REPLICAS * TP, ROWS, 128), AXES, 0, 0, tiled=True
    ).reshape(N_REP, N_HEAD, ROWS, 128)
    return pl.pallas_call(
        unpack_kernel,
        out_shape=jax.ShapeDtypeStruct((1, 1, N_REP, CAP, LAYERS, STEPS, N_HEAD * 128), BF16),
        in_specs=[VMEM],
        out_specs=VMEM,
        compiler_params=pltpu.CompilerParams(vmem_limit_bytes=16 << 20),
        name="unpack",
    )(back)


def solution(mesh):
    return jax.shard_map(
        shards,
        mesh=mesh,
        in_specs=(
            P("rep", None, "head", None, None),
            P("rep", None, None, "head"),
            P("rep", None, None, None),
            P("rep", None),
            P("rep", "head", None, None, None, None, None),
            P("rep", None, None, None, None, None, None),
            P("rep", "head", None, None, None, None, None),
            P(),
            P(),
            P(),
            P(),
            P(),
            P(),
            P(),
        ),
        out_specs=P("rep", "head", None, None, None, None, None),
        check_vma=False,
    )
```

```python
import jax
import jax.numpy as jnp
from jax import lax
from jax.experimental import pallas as pl
from jax.experimental.pallas import tpu as pltpu
from jax.sharding import PartitionSpec as P

F32 = jnp.float32
BF16 = jnp.bfloat16
AXES = ("head", "rep")
N_REP, N_HEAD, TP, CAP, LAYERS, STEPS, KERNEL = 8, 16, 4, 2, 2, 2, 4
SUBS = N_HEAD // TP
REPLICAS = N_REP * SUBS
REQ = 32
HEADS = 128
HEADS_LOCAL = HEADS // N_HEAD
HEAD_DIM, STATE = 64, 128
WIDTH = HEADS_LOCAL * HEAD_DIM
RANK_WIDTH = WIDTH // TP
GROUP_SPAN = 1024
ROWS = CAP * LAYERS * STEPS
PAIRS = CAP * LAYERS + 3
SLOT_ROWS = REPLICAS * ROWS
FAR = 14
NEAR = REQ - FAR
PIECE = 7
HIST_ROWS = REQ * (KERNEL - 1) * LAYERS
VMEM = pl.BlockSpec(memory_space=pltpu.VMEM)
SMEM = pl.BlockSpec(memory_space=pltpu.SMEM)
HBM = pl.BlockSpec(memory_space=pltpu.HBM)


def iota(shape, dim):
    return lax.broadcasted_iota(jnp.int32, shape, dim)


def one_hot(cond):
    return jnp.where(cond, 1.0, 0.0).astype(BF16)


def dot(a, b):
    return jnp.dot(a, b, preferred_element_type=F32)


def split3(v):
    hi = v.astype(BF16)
    rest = v - hi.astype(F32)
    mid = rest.astype(BF16)
    return hi, mid, (rest - mid.astype(F32)).astype(BF16)


def pack_kernel(
    inner_hbm,
    group_hbm,
    rate_hbm,
    inner_tail_hbm,
    group_tail_hbm,
    chosen_hbm,
    conv_inner_hbm,
    conv_group_hbm,
    bias_inner_hbm,
    bias_group_hbm,
    rate_bias_hbm,
    decay_hbm,
    skip_hbm,
    states_hbm,
    out_ref,
    states_ref,
    slots_ref,
    part_ref,
    taps_ref,
    params_ref,
    inner_buf,
    group_buf,
    rate_ref,
    rate_buf,
    hist_buf,
    inner_tail_ref,
    tail_b_ref,
    tail_c_ref,
    chosen_ref,
    conv_inner_ref,
    conv_b_ref,
    conv_c_ref,
    bias_inner_ref,
    bias_b_ref,
    bias_c_ref,
    rate_bias_ref,
    decay_ref,
    skip_ref,
    listing,
    counts,
    sems,
):
    pos = lax.axis_index("head")
    sub, rank = lax.div(pos, TP), lax.rem(pos, TP)
    quarter = group_hbm.at[0, sub, :, lax.div(rank, LAYERS), lax.rem(rank, LAYERS)]
    copies = [
        pltpu.make_async_copy(src, dst, sems.at[13 + n])
        for n, (src, dst) in enumerate(
            ((rate_hbm.at[0, 0], rate_ref), (quarter, group_buf), (inner_hbm.at[0, 0], inner_buf))
        )
    ]
    for copy in copies:
        copy.start()
    inner = pl.ds(pl.multiple_of(pos * WIDTH, WIDTH), WIDTH)
    b = pl.ds(pl.multiple_of(lax.div(pos, 2) * STATE, STATE), STATE)
    c = pl.ds(pl.multiple_of(GROUP_SPAN + lax.div(pos, 2) * STATE, STATE), STATE)
    moves = (
        (chosen_hbm, chosen_ref),
        (inner_tail_hbm, inner_tail_ref),
        (group_tail_hbm.at[:, :, :, b], tail_b_ref),
        (group_tail_hbm.at[:, :, :, c], tail_c_ref),
        (conv_inner_hbm.at[:, :, inner], conv_inner_ref),
        (conv_group_hbm.at[:, :, b], conv_b_ref),
        (conv_group_hbm.at[:, :, c], conv_c_ref),
        (bias_inner_hbm.at[:, inner], bias_inner_ref),
        (bias_group_hbm.at[:, b], bias_b_ref),
        (bias_group_hbm.at[:, c], bias_c_ref),
        (rate_bias_hbm, rate_bias_ref),
        (decay_hbm, decay_ref),
        (skip_hbm, skip_ref),
    )
    tails = [pltpu.make_async_copy(src, dst, sems.at[n]) for n, (src, dst) in enumerate(moves)]
    for copy in tails:
        copy.start()
    listed = pltpu.make_async_copy(chosen_hbm, listing, sems.at[17])
    listed.start()
    near = pltpu.make_async_copy(states_hbm.at[pl.ds(0, NEAR * LAYERS)], states_ref, sems.at[16])
    near.start()

    @pl.loop(0, REPLICAS)
    def _(q):
        counts[q] = 0

    copies[0].wait()
    for r in range(N_REP):
        rate_buf[r * ROWS : (r + 1) * ROWS] = jnp.concatenate(
            [rate_ref[r, c, l].astype(F32) for c in range(CAP) for l in range(LAYERS)], axis=0
        )
    rates = rate_buf[...].astype(BF16)
    rate_rows = jnp.zeros((N_HEAD, N_REP * 128), F32)
    for u in range(2):
        pick = one_hot(iota((N_HEAD, 2 * N_HEAD), 1) == 2 * iota((N_HEAD, 2 * N_HEAD), 0) + u)
        turned = lax.dot_general(
            pick, rates, (((1,), (1,)), ((), ())), preferred_element_type=F32
        ).astype(BF16)
        shape = (N_REP * ROWS, N_REP * 128)
        row, lane = iota(shape, 0), iota(shape, 1)
        place = one_hot(
            (row // ROWS == lane // 128) & (lane % 128 == 2 * (row % ROWS) + u)
        )
        rate_rows = rate_rows + dot(turned, place)
    copies[1].wait()
    copies[2].wait()
    for r in range(N_REP):
        fresh = group_buf[r]
        inner = [inner_buf[r, c, l] for c in range(CAP) for l in range(LAYERS)]
        for h in range(N_HEAD):
            for m in range(CAP * LAYERS):
                out_ref[h, r, m] = inner[m][:, h * 128 : (h + 1) * 128]
            at = (h // 2) * 128
            out_ref[h, r, 4] = fresh[:, at : at + 128]
            out_ref[h, r, 5] = fresh[:, GROUP_SPAN + at : GROUP_SPAN + at + 128]
            out_ref[h, r, 6] = jnp.broadcast_to(
                rate_rows[h : h + 1, r * 128 : (r + 1) * 128], (2, 128)
            ).astype(BF16)
    for copy in tails:
        copy.wait()
    for i in range(REQ):
        for j in range(KERNEL - 1):
            rows = slice((i * 3 + j) * 2, (i * 3 + j) * 2 + 2)
            hist_buf[rows, 0:WIDTH] = inner_tail_ref[i, j].astype(F32)
            hist_buf[rows, WIDTH : WIDTH + STATE] = tail_b_ref[i, j].astype(F32)
            hist_buf[rows, WIDTH + STATE :] = tail_c_ref[i, j].astype(F32)
    listed.wait()
    for i in range(REQ):
        q = listing[0, i]
        rank = counts[q]
        slots_ref[i] = CAP * q + rank
        counts[q] = rank + 1
    chosen = chosen_ref[...].astype(F32)
    ri, ci = iota((REQ, REQ), 0), iota((REQ, REQ), 1)
    column = jnp.sum(jnp.where(ri == ci, chosen, 0.0), axis=1, keepdims=True)
    before = jnp.where((column == chosen) & (ri < ci), 1.0, 0.0)
    slots = CAP * chosen + jnp.sum(before, axis=0, keepdims=True)
    slots = jnp.broadcast_to(slots, (8, REQ)).astype(BF16)
    wide = dot(slots, one_hot(iota((REQ, HIST_ROWS), 1) // 6 == iota((REQ, HIST_ROWS), 0)))[0:1]
    col = iota((1, HIST_ROWS), 1)
    col_key = wide.astype(jnp.int32) * 8 + (col % 2) * 4 + (col % 6) // 2
    row = iota((SLOT_ROWS, HIST_ROWS), 0)
    row_key = (row // 4) * 8 + ((row // 2) % 2) * 4 + row % 2
    hist = hist_buf[...].astype(BF16)
    second = (iota((ROWS, 1), 0) // 2) % 2 == 1
    later = iota((ROWS, 1), 0) % 2 == 1

    def by_layer(first, other):
        return jnp.where(second, other, first)

    def weight(tap):
        rows = [ref[:, tap : tap + 1, :] for ref in (conv_inner_ref, conv_b_ref, conv_c_ref)]
        return jnp.concatenate([by_layer(w[0], w[1]) for w in rows], axis=1)

    offset = jnp.concatenate(
        [by_layer(ref[0:1], ref[1:2]) for ref in (bias_inner_ref, bias_b_ref, bias_c_ref)], axis=1
    )
    total = jnp.broadcast_to(offset[None], (REPLICAS, ROWS, WIDTH + 2 * STATE))
    for tap in range(KERNEL - 1):
        window = dot(one_hot(row_key + tap == col_key), hist)
        total = total + weight(tap)[None] * window.reshape(REPLICAS, ROWS, WIDTH + 2 * STATE)
    part_ref[...] = total
    taps_ref[0] = jnp.where(later, weight(2), 0.0)
    taps_ref[1] = weight(3)
    spread = one_hot(
        iota((HEADS, WIDTH), 0) == pos * HEADS_LOCAL + iota((HEADS, WIDTH), 1) // HEAD_DIM
    )
    for n, ref in enumerate((rate_bias_ref, decay_ref, skip_ref)):
        both = by_layer(ref[0:1], ref[1:2])
        hi, mid, lo = split3(both)
        value = dot(hi, spread) + dot(mid, spread) + dot(lo, spread)
        params_ref[n] = jnp.exp(value) if n == 1 else value
    near.wait()


def step_kernel(
    got_ref,
    near_ref,
    states_hbm,
    slots_ref,
    part_ref,
    taps_ref,
    params_ref,
    out_ref,
    read_buf,
    dots_buf,
    product_buf,
    base_buf,
    gain_buf,
    far_buf,
    sems,
):
    def fetch(n):
        return pltpu.make_async_copy(
            states_hbm.at[pl.ds((NEAR + n * PIECE) * LAYERS, PIECE * LAYERS)],
            far_buf.at[pl.ds(n * PIECE * LAYERS, PIECE * LAYERS)],
            sems.at[n],
        )

    @pl.loop(0, FAR // PIECE)
    def _(n):
        fetch(n).start()

    later = iota((1, ROWS, 128), 1) % 2 == 1
    layer = (iota((1, 2 * ROWS, 128), 1) // STEPS) % LAYERS
    tap2_b = taps_ref[0, :, WIDTH : WIDTH + STATE][None]
    tap2_c = taps_ref[0, :, WIDTH + STATE :][None]
    tap3_b = taps_ref[1, :, WIDTH : WIDTH + STATE][None]
    tap3_c = taps_ref[1, :, WIDTH + STATE :][None]
    group = 4
    for q in range(0, REPLICAS, group):
        b_new, c_new = [
            jnp.concatenate([got_ref[:, t, q // SUBS, m].astype(F32) for t in range(TP)], axis=1)
            for m in (4, 5)
        ]
        b_act = part_ref[q : q + group, :, WIDTH : WIDTH + STATE]
        c_act = part_ref[q : q + group, :, WIDTH + STATE :]
        b_act = b_act + tap2_b * pltpu.roll(b_new, 1, 1) + tap3_b * b_new
        c_act = c_act + tap2_c * pltpu.roll(c_new, 1, 1) + tap3_c * c_new
        b_act = b_act * jax.nn.sigmoid(b_act)
        c_act = c_act * jax.nn.sigmoid(c_act)
        hi = c_act.astype(BF16).astype(F32)
        both = jnp.concatenate([hi, c_act - hi], axis=1)
        halves = [jnp.where(layer == l, both, 0.0) for l in range(LAYERS)]
        read_buf[q : q + group] = jnp.concatenate(halves, axis=2).astype(BF16)
        same = jnp.sum(b_act * c_act, axis=2, keepdims=True)
        cross = jnp.sum(pltpu.roll(b_act, 1, 1) * c_act, axis=2, keepdims=True)
        dots_buf[0, q : q + group] = jnp.broadcast_to(same, (group, ROWS, 128))
        dots_buf[1, q : q + group] = jnp.broadcast_to(cross, (group, ROWS, 128))
    product_buf[...] = jnp.zeros_like(product_buf)
    row, lane = iota((ROWS, 128), 0), iota((ROWS, 128), 1)
    mine = lane // 2 == row
    spread = one_hot(
        (iota((128, 128), 0) % 2 == iota((128, 128), 1) // HEAD_DIM) & (iota((128, 128), 0) < 16)
    )

    def rest(t, q):
        lanes = slice(t * RANK_WIDTH, (t + 1) * RANK_WIDTH)
        tap2, tap3 = taps_ref[0, :, lanes][None], taps_ref[1, :, lanes][None]
        raw = got_ref[:, t, q // SUBS, 6].astype(F32)[:, 0:1, :]
        raw = jnp.where(mine[None], raw, 0.0).astype(BF16).reshape(group * ROWS, 128)
        rate = dot(raw, spread).reshape(group, ROWS, 128) + params_ref[0, :, lanes][None]
        dt = jnp.maximum(rate, 0.0) + jnp.log1p(jnp.exp(-jnp.abs(rate)))
        damp = jnp.exp(-dt * params_ref[1, :, lanes][None])
        fresh = jnp.concatenate(
            [got_ref[:, t, q // SUBS, m].astype(F32) for m in range(CAP * LAYERS)], axis=1
        )
        x = part_ref[q : q + group, :, lanes]
        x = x + tap2 * pltpu.roll(fresh, 1, 1) + tap3 * fresh
        x = x * jax.nn.sigmoid(x)
        taken = dt * x
        before = jnp.where(later, pltpu.roll(damp, 1, 1), 1.0)
        carried = jnp.where(later, pltpu.roll(taken, 1, 1) * dots_buf[1, q : q + group], 0.0)
        gain_buf[q : q + group, :, lanes] = damp * before
        base_buf[q : q + group, :, lanes] = (
            damp * carried + taken * dots_buf[0, q : q + group] + params_ref[2, :, lanes][None] * x
        )

    parts = [(t, q) for q in range(0, REPLICAS, group) for t in range(TP)]
    rank_of_row = iota((ROWS, WIDTH), 0) // (LAYERS * STEPS)
    for i in range(REQ):
        q, rank = lax.shift_right_logical(slots_ref[i], 1), slots_ref[i] & 1
        if i >= NEAR and (i - NEAR) % PIECE == 0:
            fetch((i - NEAR) // PIECE).wait()
        state = near_ref if i < NEAR else far_buf
        at = (i if i < NEAR else i - NEAR) * LAYERS
        state = jnp.concatenate([state[at + l] for l in range(LAYERS)], axis=1)
        prod = lax.dot_general(
            read_buf[q], state, (((1,), (1,)), ((), ())), preferred_element_type=F32
        )
        prod = prod[0:ROWS] + prod[ROWS:]
        product_buf[q] = product_buf[q] + jnp.where(rank_of_row == rank, prod, 0.0)
        rest(*parts[i])
    for q in range(0, REPLICAS, group):
        for t in range(TP):
            lanes = slice(t * RANK_WIDTH, (t + 1) * RANK_WIDTH)
            y = base_buf[q : q + group, :, lanes]
            y = y + gain_buf[q : q + group, :, lanes] * product_buf[q : q + group, :, lanes]
            out_ref[:, t, q // SUBS] = y.astype(BF16)


def unpack_kernel(got_ref, out_ref):
    for r in range(N_REP):
        rows = jnp.concatenate([got_ref[h, r].astype(F32) for h in range(N_HEAD)], axis=1)
        for c in range(CAP):
            for l in range(LAYERS):
                at = (c * LAYERS + l) * STEPS
                out_ref[0, 0, r, c, l] = rows[at : at + STEPS].astype(BF16)


def shards(
    prefill_states,
    inner_tail,
    group_tail,
    assignment,
    decode_inner,
    decode_groups,
    decode_rate,
    conv_inner,
    conv_group,
    bias_inner,
    bias_group,
    rate_bias,
    decay_log,
    skip_gain,
):
    states = pltpu.with_memory_space_constraint(
        prefill_states.reshape(REQ * LAYERS, WIDTH, STATE), pltpu.HBM
    )
    chosen = pltpu.with_memory_space_constraint(assignment.reshape(1, REQ), pltpu.HBM)
    tail = (REQ, KERNEL - 1, LAYERS)
    packed, near, slots, part, taps, params = pl.pallas_call(
        pack_kernel,
        out_shape=(
            jax.ShapeDtypeStruct((N_HEAD, N_REP, PAIRS, 2, 128), BF16),
            jax.ShapeDtypeStruct((NEAR * LAYERS, WIDTH, STATE), BF16),
            pltpu.SMEM((REQ,), jnp.int32),
            jax.ShapeDtypeStruct((REPLICAS, ROWS, WIDTH + 2 * STATE), F32),
            jax.ShapeDtypeStruct((2, ROWS, WIDTH + 2 * STATE), F32),
            jax.ShapeDtypeStruct((3, ROWS, WIDTH), F32),
        ),
        in_specs=[HBM] * 14,
        out_specs=(VMEM, VMEM, SMEM, VMEM, VMEM, VMEM),
        scratch_shapes=[
            pltpu.VMEM(decode_inner.shape[2:], BF16),
            pltpu.VMEM((N_REP, STEPS, 2 * GROUP_SPAN), BF16),
            pltpu.VMEM(decode_rate.shape[2:], BF16),
            pltpu.VMEM((N_REP * ROWS, 2 * N_HEAD), F32),
            pltpu.VMEM((HIST_ROWS, WIDTH + 2 * STATE), F32),
            pltpu.VMEM(tail + (WIDTH,), BF16),
            pltpu.VMEM(tail + (STATE,), BF16),
            pltpu.VMEM(tail + (STATE,), BF16),
            pltpu.VMEM((1, REQ), jnp.int32),
            pltpu.VMEM((LAYERS, KERNEL, WIDTH), F32),
            pltpu.VMEM((LAYERS, KERNEL, STATE), F32),
            pltpu.VMEM((LAYERS, KERNEL, STATE), F32),
            pltpu.VMEM((LAYERS, WIDTH), F32),
            pltpu.VMEM((LAYERS, STATE), F32),
            pltpu.VMEM((LAYERS, STATE), F32),
            pltpu.VMEM((LAYERS, HEADS), F32),
            pltpu.VMEM((LAYERS, HEADS), F32),
            pltpu.VMEM((LAYERS, HEADS), F32),
            pltpu.SMEM((1, REQ), jnp.int32),
            pltpu.SMEM((REPLICAS,), jnp.int32),
            pltpu.SemaphoreType.DMA((18,)),
        ],
        compiler_params=pltpu.CompilerParams(vmem_limit_bytes=16 << 20),
        name="pack",
    )(
        *[
            pltpu.with_memory_space_constraint(v, pltpu.HBM)
            for v in (
                decode_inner,
                decode_groups,
                decode_rate,
                inner_tail.transpose(0, 2, 1, 3),
                group_tail.transpose(0, 2, 1, 3),
                chosen,
                conv_inner,
                conv_group,
                bias_inner,
                bias_group,
                rate_bias,
                decay_log,
                skip_gain,
                states,
            )
        ]
    )
    got = lax.all_to_all(
        packed.reshape(N_HEAD * N_REP, PAIRS, 2, 128), AXES, 0, 0, tiled=True
    ).reshape(SUBS, TP, N_REP, PAIRS, 2, 128)
    decoded = pl.pallas_call(
        step_kernel,
        out_shape=jax.ShapeDtypeStruct((SUBS, TP, N_REP, ROWS, 128), BF16),
        in_specs=[VMEM, VMEM, HBM, SMEM, VMEM, VMEM, VMEM],
        out_specs=VMEM,
        scratch_shapes=[
            pltpu.VMEM((REPLICAS, 2 * ROWS, LAYERS * STATE), BF16),
            pltpu.VMEM((2, REPLICAS, ROWS, 128), F32),
            pltpu.VMEM((REPLICAS, ROWS, WIDTH), F32),
            pltpu.VMEM((REPLICAS, ROWS, WIDTH), F32),
            pltpu.VMEM((REPLICAS, ROWS, WIDTH), F32),
            pltpu.VMEM((max(FAR, 1) * LAYERS, WIDTH, STATE), BF16),
            pltpu.SemaphoreType.DMA((FAR // PIECE,)),
        ],
        compiler_params=pltpu.CompilerParams(vmem_limit_bytes=20 << 20),
        name="step",
    )(got, near, states, slots, part, taps, params)
    back = lax.all_to_all(
        decoded.reshape(N_HEAD * N_REP, ROWS, 128), AXES, 0, 0, tiled=True
    ).reshape(N_HEAD, N_REP, ROWS, 128)
    return pl.pallas_call(
        unpack_kernel,
        out_shape=jax.ShapeDtypeStruct((1, 1, N_REP, CAP, LAYERS, STEPS, N_HEAD * 128), BF16),
        in_specs=[VMEM],
        out_specs=VMEM,
        compiler_params=pltpu.CompilerParams(vmem_limit_bytes=16 << 20),
        name="unpack",
    )(back)


def solution(mesh):
    return jax.shard_map(
        shards,
        mesh=mesh,
        in_specs=(
            P("rep", None, "head", None, None),
            P("rep", None, None, "head"),
            P("rep", None, None, None),
            P("rep", None),
            P("rep", "head", None, None, None, None, None),
            P("rep", None, None, None, None, None, None),
            P("rep", "head", None, None, None, None, None),
            P(),
            P(),
            P(),
            P(),
            P(),
            P(),
            P(),
        ),
        out_specs=P("rep", "head", None, None, None, None, None),
        check_vma=False,
    )
```

```python
import jax
import jax.numpy as jnp
from jax import lax
from jax.experimental import pallas as pl
from jax.experimental.pallas import tpu as pltpu
from jax.sharding import PartitionSpec as P

F32 = jnp.float32
BF16 = jnp.bfloat16
AXES = ("head", "rep")
N_REP, N_HEAD, TP, CAP, LAYERS, STEPS, KERNEL = 8, 16, 4, 2, 2, 2, 4
SUBS = N_HEAD // TP
REPLICAS = N_REP * SUBS
REQ = 32
HEADS = 128
HEADS_LOCAL = HEADS // N_HEAD
HEAD_DIM, STATE = 64, 128
WIDTH = HEADS_LOCAL * HEAD_DIM
RANK_WIDTH = WIDTH // TP
GROUP_SPAN = 1024
ROWS = CAP * LAYERS * STEPS
PAIRS = CAP * LAYERS + 3
SLOT_ROWS = REPLICAS * ROWS
FAR = 14
NEAR = REQ - FAR
PIECE = 2
WAITS = {0: (0, 1, 2, 3), 8: (4, 5, 6)}
HIST_ROWS = REQ * (KERNEL - 1) * LAYERS
VMEM = pl.BlockSpec(memory_space=pltpu.VMEM)
SMEM = pl.BlockSpec(memory_space=pltpu.SMEM)
HBM = pl.BlockSpec(memory_space=pltpu.HBM)


def iota(shape, dim):
    return lax.broadcasted_iota(jnp.int32, shape, dim)


def one_hot(cond):
    return jnp.where(cond, 1.0, 0.0).astype(BF16)


def dot(a, b):
    return jnp.dot(a, b, preferred_element_type=F32)


def split3(v):
    hi = v.astype(BF16)
    rest = v - hi.astype(F32)
    mid = rest.astype(BF16)
    return hi, mid, (rest - mid.astype(F32)).astype(BF16)


def pack_kernel(
    inner_hbm,
    group_hbm,
    rate_hbm,
    inner_tail_hbm,
    group_tail_hbm,
    chosen_hbm,
    conv_inner_hbm,
    conv_group_hbm,
    bias_inner_hbm,
    bias_group_hbm,
    rate_bias_hbm,
    decay_hbm,
    skip_hbm,
    states_hbm,
    out_ref,
    states_ref,
    slots_ref,
    part_ref,
    taps_ref,
    params_ref,
    inner_buf,
    group_buf,
    rate_ref,
    rate_buf,
    hist_buf,
    inner_tail_ref,
    tail_b_ref,
    tail_c_ref,
    chosen_ref,
    conv_inner_ref,
    conv_b_ref,
    conv_c_ref,
    bias_inner_ref,
    bias_b_ref,
    bias_c_ref,
    rate_bias_ref,
    decay_ref,
    skip_ref,
    listing,
    counts,
    sems,
):
    pos = lax.axis_index("head")
    sub, rank = lax.div(pos, TP), lax.rem(pos, TP)
    quarter = group_hbm.at[0, sub, :, lax.div(rank, LAYERS), lax.rem(rank, LAYERS)]
    copies = [
        pltpu.make_async_copy(src, dst, sems.at[13 + n])
        for n, (src, dst) in enumerate(
            ((rate_hbm.at[0, 0], rate_ref), (quarter, group_buf), (inner_hbm.at[0, 0], inner_buf))
        )
    ]
    for copy in copies:
        copy.start()
    inner = pl.ds(pl.multiple_of(pos * WIDTH, WIDTH), WIDTH)
    b = pl.ds(pl.multiple_of(lax.div(pos, 2) * STATE, STATE), STATE)
    c = pl.ds(pl.multiple_of(GROUP_SPAN + lax.div(pos, 2) * STATE, STATE), STATE)
    moves = (
        (chosen_hbm, chosen_ref),
        (inner_tail_hbm, inner_tail_ref),
        (group_tail_hbm.at[:, :, :, b], tail_b_ref),
        (group_tail_hbm.at[:, :, :, c], tail_c_ref),
        (conv_inner_hbm.at[:, :, inner], conv_inner_ref),
        (conv_group_hbm.at[:, :, b], conv_b_ref),
        (conv_group_hbm.at[:, :, c], conv_c_ref),
        (bias_inner_hbm.at[:, inner], bias_inner_ref),
        (bias_group_hbm.at[:, b], bias_b_ref),
        (bias_group_hbm.at[:, c], bias_c_ref),
        (rate_bias_hbm, rate_bias_ref),
        (decay_hbm, decay_ref),
        (skip_hbm, skip_ref),
    )
    tails = [pltpu.make_async_copy(src, dst, sems.at[n]) for n, (src, dst) in enumerate(moves)]
    for copy in tails:
        copy.start()
    listed = pltpu.make_async_copy(chosen_hbm, listing, sems.at[17])
    listed.start()
    near = pltpu.make_async_copy(states_hbm.at[pl.ds(0, NEAR * LAYERS)], states_ref, sems.at[16])
    near.start()

    @pl.loop(0, REPLICAS)
    def _(q):
        counts[q] = 0

    copies[0].wait()
    for r in range(N_REP):
        rate_buf[r * ROWS : (r + 1) * ROWS] = jnp.concatenate(
            [rate_ref[r, c, l].astype(F32) for c in range(CAP) for l in range(LAYERS)], axis=0
        )
    rates = rate_buf[...].astype(BF16)
    rate_rows = jnp.zeros((N_HEAD, N_REP * 128), F32)
    for u in range(2):
        pick = one_hot(iota((N_HEAD, 2 * N_HEAD), 1) == 2 * iota((N_HEAD, 2 * N_HEAD), 0) + u)
        turned = lax.dot_general(
            pick, rates, (((1,), (1,)), ((), ())), preferred_element_type=F32
        ).astype(BF16)
        shape = (N_REP * ROWS, N_REP * 128)
        row, lane = iota(shape, 0), iota(shape, 1)
        place = one_hot(
            (row // ROWS == lane // 128) & (lane % 128 == 2 * (row % ROWS) + u)
        )
        rate_rows = rate_rows + dot(turned, place)
    copies[1].wait()
    copies[2].wait()
    for r in range(N_REP):
        fresh = group_buf[r]
        inner = [inner_buf[r, c, l] for c in range(CAP) for l in range(LAYERS)]
        for h in range(N_HEAD):
            for m in range(CAP * LAYERS):
                out_ref[h, r, m] = inner[m][:, h * 128 : (h + 1) * 128]
            at = (h // 2) * 128
            out_ref[h, r, 4] = fresh[:, at : at + 128]
            out_ref[h, r, 5] = fresh[:, GROUP_SPAN + at : GROUP_SPAN + at + 128]
            out_ref[h, r, 6] = jnp.broadcast_to(
                rate_rows[h : h + 1, r * 128 : (r + 1) * 128], (2, 128)
            ).astype(BF16)
    for copy in tails:
        copy.wait()
    for i in range(REQ):
        for j in range(KERNEL - 1):
            rows = slice((i * 3 + j) * 2, (i * 3 + j) * 2 + 2)
            hist_buf[rows, 0:WIDTH] = inner_tail_ref[i, j].astype(F32)
            hist_buf[rows, WIDTH : WIDTH + STATE] = tail_b_ref[i, j].astype(F32)
            hist_buf[rows, WIDTH + STATE :] = tail_c_ref[i, j].astype(F32)
    listed.wait()
    for i in range(REQ):
        q = listing[0, i]
        rank = counts[q]
        slots_ref[i] = CAP * q + rank
        counts[q] = rank + 1
    chosen = chosen_ref[...].astype(F32)
    ri, ci = iota((REQ, REQ), 0), iota((REQ, REQ), 1)
    column = jnp.sum(jnp.where(ri == ci, chosen, 0.0), axis=1, keepdims=True)
    before = jnp.where((column == chosen) & (ri < ci), 1.0, 0.0)
    slots = CAP * chosen + jnp.sum(before, axis=0, keepdims=True)
    slots = jnp.broadcast_to(slots, (8, REQ)).astype(BF16)
    wide = dot(slots, one_hot(iota((REQ, HIST_ROWS), 1) // 6 == iota((REQ, HIST_ROWS), 0)))[0:1]
    col = iota((1, HIST_ROWS), 1)
    col_key = wide.astype(jnp.int32) * 8 + (col % 2) * 4 + (col % 6) // 2
    row = iota((SLOT_ROWS, HIST_ROWS), 0)
    row_key = (row // 4) * 8 + ((row // 2) % 2) * 4 + row % 2
    hist = hist_buf[...].astype(BF16)
    second = (iota((ROWS, 1), 0) // 2) % 2 == 1
    later = iota((ROWS, 1), 0) % 2 == 1

    def by_layer(first, other):
        return jnp.where(second, other, first)

    def weight(tap):
        rows = [ref[:, tap : tap + 1, :] for ref in (conv_inner_ref, conv_b_ref, conv_c_ref)]
        return jnp.concatenate([by_layer(w[0], w[1]) for w in rows], axis=1)

    offset = jnp.concatenate(
        [by_layer(ref[0:1], ref[1:2]) for ref in (bias_inner_ref, bias_b_ref, bias_c_ref)], axis=1
    )
    total = jnp.broadcast_to(offset[None], (REPLICAS, ROWS, WIDTH + 2 * STATE))
    for tap in range(KERNEL - 1):
        window = dot(one_hot(row_key + tap == col_key), hist)
        total = total + weight(tap)[None] * window.reshape(REPLICAS, ROWS, WIDTH + 2 * STATE)
    part_ref[...] = total
    taps_ref[0] = jnp.where(later, weight(2), 0.0)
    taps_ref[1] = weight(3)
    spread = one_hot(
        iota((HEADS, WIDTH), 0) == pos * HEADS_LOCAL + iota((HEADS, WIDTH), 1) // HEAD_DIM
    )
    for n, ref in enumerate((rate_bias_ref, decay_ref, skip_ref)):
        both = by_layer(ref[0:1], ref[1:2])
        hi, mid, lo = split3(both)
        value = dot(hi, spread) + dot(mid, spread) + dot(lo, spread)
        params_ref[n] = jnp.exp(value) if n == 1 else value
    near.wait()


def step_kernel(
    got_ref,
    near_ref,
    states_hbm,
    slots_ref,
    part_ref,
    taps_ref,
    params_ref,
    out_ref,
    read_buf,
    dots_buf,
    product_buf,
    base_buf,
    gain_buf,
    far_buf,
    sems,
):
    def fetch(n):
        return pltpu.make_async_copy(
            states_hbm.at[pl.ds((NEAR + n * PIECE) * LAYERS, PIECE * LAYERS)],
            far_buf.at[pl.ds(n * PIECE * LAYERS, PIECE * LAYERS)],
            sems.at[n],
        )

    @pl.loop(0, FAR // PIECE)
    def _(n):
        fetch(n).start()

    later = iota((1, ROWS, 128), 1) % 2 == 1
    layer = (iota((1, 2 * ROWS, 128), 1) // STEPS) % LAYERS
    tap2_b = taps_ref[0, :, WIDTH : WIDTH + STATE][None]
    tap2_c = taps_ref[0, :, WIDTH + STATE :][None]
    tap3_b = taps_ref[1, :, WIDTH : WIDTH + STATE][None]
    tap3_c = taps_ref[1, :, WIDTH + STATE :][None]
    group = 4
    for q in range(0, REPLICAS, group):
        b_new, c_new = [
            jnp.concatenate([got_ref[:, t, q // SUBS, m].astype(F32) for t in range(TP)], axis=1)
            for m in (4, 5)
        ]
        b_act = part_ref[q : q + group, :, WIDTH : WIDTH + STATE]
        c_act = part_ref[q : q + group, :, WIDTH + STATE :]
        b_act = b_act + tap2_b * pltpu.roll(b_new, 1, 1) + tap3_b * b_new
        c_act = c_act + tap2_c * pltpu.roll(c_new, 1, 1) + tap3_c * c_new
        b_act = b_act * jax.nn.sigmoid(b_act)
        c_act = c_act * jax.nn.sigmoid(c_act)
        hi = c_act.astype(BF16).astype(F32)
        both = jnp.concatenate([hi, c_act - hi], axis=1)
        halves = [jnp.where(layer == l, both, 0.0) for l in range(LAYERS)]
        read_buf[q : q + group] = jnp.concatenate(halves, axis=2).astype(BF16)
        same = jnp.sum(b_act * c_act, axis=2, keepdims=True)
        cross = jnp.sum(pltpu.roll(b_act, 1, 1) * c_act, axis=2, keepdims=True)
        dots_buf[0, q : q + group] = jnp.broadcast_to(same, (group, ROWS, 128))
        dots_buf[1, q : q + group] = jnp.broadcast_to(cross, (group, ROWS, 128))
    product_buf[...] = jnp.zeros_like(product_buf)
    row, lane = iota((ROWS, 128), 0), iota((ROWS, 128), 1)
    mine = lane // 2 == row
    spread = one_hot(
        (iota((128, 128), 0) % 2 == iota((128, 128), 1) // HEAD_DIM) & (iota((128, 128), 0) < 16)
    )

    def rest(t, q):
        lanes = slice(t * RANK_WIDTH, (t + 1) * RANK_WIDTH)
        tap2, tap3 = taps_ref[0, :, lanes][None], taps_ref[1, :, lanes][None]
        raw = got_ref[:, t, q // SUBS, 6].astype(F32)[:, 0:1, :]
        raw = jnp.where(mine[None], raw, 0.0).astype(BF16).reshape(group * ROWS, 128)
        rate = dot(raw, spread).reshape(group, ROWS, 128) + params_ref[0, :, lanes][None]
        dt = jnp.maximum(rate, 0.0) + jnp.log1p(jnp.exp(-jnp.abs(rate)))
        damp = jnp.exp(-dt * params_ref[1, :, lanes][None])
        fresh = jnp.concatenate(
            [got_ref[:, t, q // SUBS, m].astype(F32) for m in range(CAP * LAYERS)], axis=1
        )
        x = part_ref[q : q + group, :, lanes]
        x = x + tap2 * pltpu.roll(fresh, 1, 1) + tap3 * fresh
        x = x * jax.nn.sigmoid(x)
        taken = dt * x
        before = jnp.where(later, pltpu.roll(damp, 1, 1), 1.0)
        carried = jnp.where(later, pltpu.roll(taken, 1, 1) * dots_buf[1, q : q + group], 0.0)
        gain_buf[q : q + group, :, lanes] = damp * before
        base_buf[q : q + group, :, lanes] = (
            damp * carried + taken * dots_buf[0, q : q + group] + params_ref[2, :, lanes][None] * x
        )

    parts = [(t, q) for q in range(0, REPLICAS, group) for t in range(TP)]
    rank_of_row = iota((ROWS, WIDTH), 0) // (LAYERS * STEPS)
    for i in range(REQ):
        q, rank = lax.shift_right_logical(slots_ref[i], 1), slots_ref[i] & 1
        for n in WAITS.get(i - NEAR, ()):
            fetch(n).wait()
        state = near_ref if i < NEAR else far_buf
        at = (i if i < NEAR else i - NEAR) * LAYERS
        state = jnp.concatenate([state[at + l] for l in range(LAYERS)], axis=1)
        prod = lax.dot_general(
            read_buf[q], state, (((1,), (1,)), ((), ())), preferred_element_type=F32
        )
        prod = prod[0:ROWS] + prod[ROWS:]
        product_buf[q] = product_buf[q] + jnp.where(rank_of_row == rank, prod, 0.0)
        rest(*parts[i])
    for q in range(0, REPLICAS, group):
        for t in range(TP):
            lanes = slice(t * RANK_WIDTH, (t + 1) * RANK_WIDTH)
            y = base_buf[q : q + group, :, lanes]
            y = y + gain_buf[q : q + group, :, lanes] * product_buf[q : q + group, :, lanes]
            out_ref[:, t, q // SUBS] = y.astype(BF16)


def unpack_kernel(got_ref, out_ref):
    for r in range(N_REP):
        rows = jnp.concatenate([got_ref[h, r].astype(F32) for h in range(N_HEAD)], axis=1)
        for c in range(CAP):
            for l in range(LAYERS):
                at = (c * LAYERS + l) * STEPS
                out_ref[0, 0, r, c, l] = rows[at : at + STEPS].astype(BF16)


def shards(
    prefill_states,
    inner_tail,
    group_tail,
    assignment,
    decode_inner,
    decode_groups,
    decode_rate,
    conv_inner,
    conv_group,
    bias_inner,
    bias_group,
    rate_bias,
    decay_log,
    skip_gain,
):
    states = pltpu.with_memory_space_constraint(
        prefill_states.reshape(REQ * LAYERS, WIDTH, STATE), pltpu.HBM
    )
    chosen = pltpu.with_memory_space_constraint(assignment.reshape(1, REQ), pltpu.HBM)
    tail = (REQ, KERNEL - 1, LAYERS)
    packed, near, slots, part, taps, params = pl.pallas_call(
        pack_kernel,
        out_shape=(
            jax.ShapeDtypeStruct((N_HEAD, N_REP, PAIRS, 2, 128), BF16),
            jax.ShapeDtypeStruct((NEAR * LAYERS, WIDTH, STATE), BF16),
            pltpu.SMEM((REQ,), jnp.int32),
            jax.ShapeDtypeStruct((REPLICAS, ROWS, WIDTH + 2 * STATE), F32),
            jax.ShapeDtypeStruct((2, ROWS, WIDTH + 2 * STATE), F32),
            jax.ShapeDtypeStruct((3, ROWS, WIDTH), F32),
        ),
        in_specs=[HBM] * 14,
        out_specs=(VMEM, VMEM, SMEM, VMEM, VMEM, VMEM),
        scratch_shapes=[
            pltpu.VMEM(decode_inner.shape[2:], BF16),
            pltpu.VMEM((N_REP, STEPS, 2 * GROUP_SPAN), BF16),
            pltpu.VMEM(decode_rate.shape[2:], BF16),
            pltpu.VMEM((N_REP * ROWS, 2 * N_HEAD), F32),
            pltpu.VMEM((HIST_ROWS, WIDTH + 2 * STATE), F32),
            pltpu.VMEM(tail + (WIDTH,), BF16),
            pltpu.VMEM(tail + (STATE,), BF16),
            pltpu.VMEM(tail + (STATE,), BF16),
            pltpu.VMEM((1, REQ), jnp.int32),
            pltpu.VMEM((LAYERS, KERNEL, WIDTH), F32),
            pltpu.VMEM((LAYERS, KERNEL, STATE), F32),
            pltpu.VMEM((LAYERS, KERNEL, STATE), F32),
            pltpu.VMEM((LAYERS, WIDTH), F32),
            pltpu.VMEM((LAYERS, STATE), F32),
            pltpu.VMEM((LAYERS, STATE), F32),
            pltpu.VMEM((LAYERS, HEADS), F32),
            pltpu.VMEM((LAYERS, HEADS), F32),
            pltpu.VMEM((LAYERS, HEADS), F32),
            pltpu.SMEM((1, REQ), jnp.int32),
            pltpu.SMEM((REPLICAS,), jnp.int32),
            pltpu.SemaphoreType.DMA((18,)),
        ],
        compiler_params=pltpu.CompilerParams(vmem_limit_bytes=16 << 20),
        name="pack",
    )(
        *[
            pltpu.with_memory_space_constraint(v, pltpu.HBM)
            for v in (
                decode_inner,
                decode_groups,
                decode_rate,
                inner_tail.transpose(0, 2, 1, 3),
                group_tail.transpose(0, 2, 1, 3),
                chosen,
                conv_inner,
                conv_group,
                bias_inner,
                bias_group,
                rate_bias,
                decay_log,
                skip_gain,
                states,
            )
        ]
    )
    got = lax.all_to_all(
        packed.reshape(N_HEAD * N_REP, PAIRS, 2, 128), AXES, 0, 0, tiled=True
    ).reshape(SUBS, TP, N_REP, PAIRS, 2, 128)
    decoded = pl.pallas_call(
        step_kernel,
        out_shape=jax.ShapeDtypeStruct((SUBS, TP, N_REP, ROWS, 128), BF16),
        in_specs=[VMEM, VMEM, HBM, SMEM, VMEM, VMEM, VMEM],
        out_specs=VMEM,
        scratch_shapes=[
            pltpu.VMEM((REPLICAS, 2 * ROWS, LAYERS * STATE), BF16),
            pltpu.VMEM((2, REPLICAS, ROWS, 128), F32),
            pltpu.VMEM((REPLICAS, ROWS, WIDTH), F32),
            pltpu.VMEM((REPLICAS, ROWS, WIDTH), F32),
            pltpu.VMEM((REPLICAS, ROWS, WIDTH), F32),
            pltpu.VMEM((max(FAR, 1) * LAYERS, WIDTH, STATE), BF16),
            pltpu.SemaphoreType.DMA((FAR // PIECE,)),
        ],
        compiler_params=pltpu.CompilerParams(vmem_limit_bytes=20 << 20),
        name="step",
    )(got, near, states, slots, part, taps, params)
    back = lax.all_to_all(
        decoded.reshape(N_HEAD * N_REP, ROWS, 128), AXES, 0, 0, tiled=True
    ).reshape(N_HEAD, N_REP, ROWS, 128)
    return pl.pallas_call(
        unpack_kernel,
        out_shape=jax.ShapeDtypeStruct((1, 1, N_REP, CAP, LAYERS, STEPS, N_HEAD * 128), BF16),
        in_specs=[VMEM],
        out_specs=VMEM,
        compiler_params=pltpu.CompilerParams(vmem_limit_bytes=16 << 20),
        name="unpack",
    )(back)


def solution(mesh):
    return jax.shard_map(
        shards,
        mesh=mesh,
        in_specs=(
            P("rep", None, "head", None, None),
            P("rep", None, None, "head"),
            P("rep", None, None, None),
            P("rep", None),
            P("rep", "head", None, None, None, None, None),
            P("rep", None, None, None, None, None, None),
            P("rep", "head", None, None, None, None, None),
            P(),
            P(),
            P(),
            P(),
            P(),
            P(),
            P(),
        ),
        out_specs=P("rep", "head", None, None, None, None, None),
        check_vma=False,
    )
```
